256 devices in a mesh: dp: 4 (over y_lo, core), fsdp: 64 (over z, y_hi, x).
Axes of the slice: x: 4, y: 4 (y_hi: 2, y_lo: 2; y = y_hi * 2 + y_lo), z: 8, core: 2. Of those that a mesh axis runs over, the one named last changes fastest.
Arguments:
- tokens: bfloat16 [1024, 5120], P('dp', 'fsdp'), may hold values from -6 to 6
- cotangent: bfloat16 [1024, 5120], P('dp', 'fsdp'), may hold values from -6 to 6
- pass_counts: int32 [64], replicated, may hold values from 0 to 8
- group_ids: int32 [64], replicated, may hold values from 0 to 7
- token_rollout: int32 [1024], P('dp'), may hold values from 0 to 63, never falling along the last dimension, each value on 1 to 32 neighbouring positions
- master_gate: float32 [13824, 5120], P('fsdp', 'dp'), may hold values from -0.078125 to 0.078125
- master_up: float32 [13824, 5120], P('fsdp', 'dp'), may hold values from -0.078125 to 0.078125
- master_down: float32 [13824, 5120], P('fsdp', 'dp'), may hold values from -0.0546875 to 0.0546875
- moment_gate: float32 [13824, 5120], P('fsdp', 'dp'), may hold values from -12 to 12
- moment_up: float32 [13824, 5120], P('fsdp', 'dp'), may hold values from -12 to 12
- moment_down: float32 [13824, 5120], P('fsdp', 'dp'), may hold values from -12 to 12
- second_gate: float32 [13824, 5120], P('fsdp', 'dp'), may hold values from 4 to 400
- second_up: float32 [13824, 5120], P('fsdp', 'dp'), may hold values from 4 to 400
- second_down: float32 [13824, 5120], P('fsdp', 'dp'), may hold values from 4 to 400
Outputs:
- block_out: bfloat16 [1024, 5120], P('dp', 'fsdp')
- grad_input: bfloat16 [1024, 5120], P('dp', 'fsdp')
- update_gate: bfloat16 [13824, 5120], P('fsdp', 'dp')
- update_up: bfloat16 [13824, 5120], P('fsdp', 'dp')
- update_down: bfloat16 [13824, 5120], P('fsdp', 'dp')
The draws below stay inside these ranges and needn't reach their ends.
Inputs may be any that keep to these rules, and one draw needn't show every extreme that they name: `token_rollout`: tokens of one rollout are consecutive, rollout numbers never fall along the tokens, and every rollout has at least one token.
All inputs are finite; a program needn't handle non-finite values.
Results may differ from the reference program's by a relative error of at most 0.008.
Values may be sent and summed in bfloat16 or wider, within the bound.
A program may use at most 128 MiB of HBM per device.

```python
import math
import jax
import jax.numpy as jnp
import numpy as np
from jax import lax

D = 5120
FF = 13824
TOKENS = 1024
ROLL = 64
GROUPS = 8
TESTS = 8


def plant(values, own_key, least, high):
    longest = values.shape.index(max(values.shape))
    spots = []
    for shift in (0, 1):
        where = [jax.random.randint(jax.random.fold_in(own_key, axis), (), 0, length) for axis, length in enumerate(values.shape)]
        where[longest] = (where[longest] + shift) % values.shape[longest]
        spots.append(tuple(where))
    return values.at[spots[0]].set(least).at[spots[1]].set(high)


def block_scale(stream_key, shape, pieces, least, high):
    factor_of = 1.0
    for axis_at, shards_of in pieces:
        draws = jax.random.uniform(jax.random.fold_in(jax.random.fold_in(stream_key, 6), axis_at), (shards_of,), jnp.float32, least / len(pieces), high / len(pieces))
        factor_of = factor_of * jnp.repeat(jnp.exp(draws), shape[axis_at] // shards_of).reshape((-1,) + (1,) * (len(shape) - 1 - axis_at))
    return factor_of


def profile(number_of, total, bound, lean):
    loads = [(1 << 20) // math.isqrt(rank ** lean) + 1 for rank in range(2, number_of + 1)]
    surplus, counts = total - bound - (number_of - 1), [1] * (number_of - 1)
    while surplus > 0:
        free = [i for i in range(number_of - 1) if counts[i] < bound]
        pool, budget = sum([loads[i] for i in free]), surplus
        for i in free:
            addition = min(bound - counts[i], max(1, budget * loads[i] // pool), surplus)
            counts[i] = counts[i] + addition
            surplus = surplus - addition
    return np.array([bound] + counts)


def uneven(rng, amount, total, most, slope):
    if amount == 2:
        one = jax.random.randint(rng, (), max(1, total - most), min(most, total - 1) + 1)
        return jnp.stack([one, total - one])
    tallies = jnp.asarray(profile(amount, total, most, slope), jnp.int32)
    pairs = (amount - 1) // 2
    giver, sink = tallies[1:1 + 2 * pairs:2], tallies[2:2 + 2 * pairs:2]
    room = jnp.minimum(giver - 1, most - sink)
    shifted = jax.random.randint(jax.random.fold_in(rng, 1), (pairs,), 0, 1 << 20) % (room + 1)
    tallies = tallies.at[1:1 + 2 * pairs:2].set(giver - shifted).at[2:2 + 2 * pairs:2].set(sink + shifted)
    return tallies[jax.random.permutation(jax.random.fold_in(rng, 2), amount)]


def normal_values(rng, extent, spread, most, shards=(), held_as=jnp.bfloat16):
    array = spread * jax.random.normal(rng, extent, jnp.float32)
    if shards:
        array = array * block_scale(rng, extent, shards, -0.22, 0.18)
    return jnp.clip(array, -most, most).astype(held_as)


def setup_inputs(seed: int = 0) -> dict:
    key_of = jax.random.split(jax.random.key(seed), 15)
    return {
        "tokens": normal_values(key_of[0], (TOKENS, D), 1.0, 6.0, ((0, 4), (1, 64))),
        "cotangent": normal_values(key_of[1], (TOKENS, D), 1.0, 6.0, ((0, 4), (1, 64))),
        "pass_counts": plant(jax.random.randint(key_of[2], (ROLL,), 0, TESTS + 1), jax.random.fold_in(key_of[2], 1), 0, TESTS).astype(jnp.int32),
        "group_ids": plant(jax.random.randint(key_of[3], (ROLL,), 0, GROUPS), jax.random.fold_in(key_of[3], 1), 0, GROUPS - 1).astype(jnp.int32),
        "token_rollout": jnp.searchsorted(jnp.cumsum(uneven(key_of[4], ROLL, TOKENS, 2 * TOKENS // ROLL, 2)), jnp.arange(TOKENS), side="right").astype(jnp.int32),
        "master_gate": normal_values(key_of[5], (FF, D), D ** -0.5, 0.078125, ((0, 64), (1, 4)), jnp.float32),
        "master_up": normal_values(key_of[6], (FF, D), D ** -0.5, 0.078125, ((0, 64), (1, 4)), jnp.float32),
        "master_down": normal_values(key_of[7], (FF, D), FF ** -0.5, 0.0546875, ((0, 64), (1, 4)), jnp.float32),
        "moment_gate": normal_values(key_of[8], (FF, D), 2.0, 12.0, ((0, 64), (1, 4)), jnp.float32),
        "moment_up": normal_values(key_of[9], (FF, D), 2.0, 12.0, ((0, 64), (1, 4)), jnp.float32),
        "moment_down": normal_values(key_of[10], (FF, D), 2.0, 12.0, ((0, 64), (1, 4)), jnp.float32),
        "second_gate": jnp.clip(jnp.exp(math.log(400.0) - 4.6051702 * jax.random.uniform(key_of[11], (FF, D), jnp.float32) ** block_scale(key_of[11], (FF, D), ((0, 64), (1, 4)), -0.2, 0.2)), 4.0, 400.0),
        "second_up": jnp.clip(jnp.exp(math.log(400.0) - 4.6051702 * jax.random.uniform(key_of[12], (FF, D), jnp.float32) ** block_scale(key_of[12], (FF, D), ((0, 64), (1, 4)), -0.2, 0.2)), 4.0, 400.0),
        "second_down": jnp.clip(jnp.exp(math.log(400.0) - 4.6051702 * jax.random.uniform(key_of[13], (FF, D), jnp.float32) ** block_scale(key_of[13], (FF, D), ((0, 64), (1, 4)), -0.2, 0.2)), 4.0, 400.0),
    }


beta_first = 0.9
beta_second = 0.95
adam_epsilon = 1e-08
weight_decay = 0.1
correct_first = 1.0 - 0.9 ** 10
correct_second = 1.0 - 0.95 ** 10

def contract(left_op, right_op, left_dim, right_dim):
    return lax.dot_general(left_op, right_op, (((left_dim,), (right_dim,)), ((), ())), preferred_element_type=jnp.float32)

def adamw(master, moment, second, gradient):
    moment_new = beta_first * moment + (1.0 - beta_first) * gradient
    second_new = beta_second * second + (1.0 - beta_second) * gradient * gradient
    result = moment_new / correct_first / (jnp.sqrt(second_new / correct_second) + adam_epsilon) + weight_decay * master
    return result.astype(jnp.bfloat16)

def reference(tokens, cotangent, pass_counts, group_ids, token_rollout, master_gate, master_up, master_down, moment_gate, moment_up, moment_down, second_gate, second_up, second_down):
    reward = pass_counts.astype(jnp.float32) / TESTS
    same_group = (group_ids[:, None] == group_ids[None, :]).astype(jnp.float32)
    baseline = lax.optimization_barrier(jnp.sum(same_group * reward[None, :], axis=1)) / lax.optimization_barrier(jnp.sum(same_group, axis=1))
    advantage = reward - baseline
    token_adv = advantage[token_rollout]
    w_gate = master_gate.astype(jnp.bfloat16)
    w_up = master_up.astype(jnp.bfloat16)
    w_down = master_down.astype(jnp.bfloat16)
    gate_in = contract(tokens, w_gate, 1, 1)
    up_in = contract(tokens, w_up, 1, 1)
    sigmoid_v = jax.nn.sigmoid(gate_in)
    active = gate_in * sigmoid_v
    slopes = sigmoid_v * (1.0 + gate_in * (1.0 - sigmoid_v))
    hidden = (active * up_in).astype(jnp.bfloat16)
    block_out = jnp.dot(hidden, w_down, preferred_element_type=jnp.float32).astype(jnp.bfloat16)
    delta_out = (-token_adv[:, None] * cotangent.astype(jnp.float32)).astype(jnp.bfloat16)
    d_hidden = contract(delta_out, w_down, 1, 1)
    d_gate = (d_hidden * up_in * slopes).astype(jnp.bfloat16)
    d_up = (d_hidden * active).astype(jnp.bfloat16)
    grad_input = (jnp.dot(d_gate, w_gate, preferred_element_type=jnp.float32) + jnp.dot(d_up, w_up, preferred_element_type=jnp.float32)).astype(jnp.bfloat16)
    grad_gate = contract(d_gate, tokens, 0, 0)
    grad_up = contract(d_up, tokens, 0, 0)
    grad_down = contract(hidden, delta_out, 0, 0)
    update_gate = adamw(master_gate, moment_gate, second_gate, grad_gate)
    update_up = adamw(master_up, moment_up, second_up, grad_up)
    update_down = adamw(master_down, moment_down, second_down, grad_down)
    return (block_out, grad_input, update_gate, update_up, update_down)
```

```python
import jax
import jax.numpy as jnp
from jax import lax
from jax.experimental import pallas as pl
from jax.experimental.pallas import tpu as pltpu
from jax.sharding import PartitionSpec as P

ROLL = 64
TESTS = 8
beta_first = 0.9
beta_second = 0.95
adam_epsilon = 1e-08
weight_decay = 0.1
correct_first = 1.0 - 0.9**10
correct_second = 1.0 - 0.95**10

FFS = 216
PAD = 224
HID = 256
DS = 1280
FB = 80
TB = 256
F32 = jnp.float32
BF16 = jnp.bfloat16


def rem(a, b):
    return lax.rem(a, jnp.int32(b))


def div(a, b):
    return lax.div(a, jnp.int32(b))


def remote(src, dst, send, recv, device):
    return pltpu.make_async_remote_copy(
        src_ref=src,
        dst_ref=dst,
        send_sem=send,
        recv_sem=recv,
        device_id=device,
        device_id_type=pl.DeviceIdType.MESH,
    )


def kernel(
    tok, dlt, mg, mu, md, og, ou, od, sg, su, sd,
    bo, gi, ug, uu, ud,
    XT, PO, RXO, RXR, RXC, ZR, YS, YR, FS, FR,
    MW, MOM, SEC, WB, WT, HD, DG, DU, GUO, ACT, US, DHO,
    SD, RD, SY, RY, SD2, RD2, SY2, RY2, GR, UO0, UO1, UO2,
    lsem, p_s, p_r, y_s, y_r, z_s, z_r, xr_s, xr_r, xl_s, xl_r, f_s, f_r,
    o_s, o_r, w_s, w_r, c_s, c_r, zz_s, zz_r, yy_s, yy_r, pp_s, pp_r,
    d_s, d_r, e_s, e_r,
):
    dp = lax.axis_index("dp")
    fs = lax.axis_index("fsdp")
    z, yh, x = div(fs, 8), rem(div(fs, 4), 2), rem(fs, 4)
    core = rem(dp, 2)
    right, left, far = rem(x + 1, 4), rem(x + 3, 4), rem(x + 2, 4)

    def at(dp_, z_, y_, x_):
        return (dp_, z_ * 8 + y_ * 4 + x_)

    d_right, d_left = at(dp, z, yh, right), at(dp, z, yh, left)
    d_y = at(dp, z, 1 - yh, x)
    home = div(z, 2)
    zq = 2 * dp + rem(z, 2)
    d_p = at(home, zq, yh, x)
    d_core = at(dp + 1 - 2 * core, z, yh, x)
    d_chip = at(rem(dp + 2, 4), z, yh, x)
    at_home = home == dp

    srcs = (mg, mu, md, og, ou, od, sg, su, sd)
    loads = []
    for n, src in enumerate(srcs):
        dst = (MW, MOM, SEC)[n // 3].at[n % 3, pl.ds(0, FFS)]
        loads.append(pltpu.make_async_copy(src, dst, lsem.at[n]))
    for load in loads:
        load.start()

    for w in range(3):
        MW[w, FFS:HID, :] = jnp.zeros((HID - FFS, DS), F32)
    for buf in (HD, DG, DU):
        for n in range(4):
            buf[n, PAD:HID, :] = jnp.zeros((HID - PAD, TB), BF16)

    barrier = pltpu.get_barrier_semaphore()
    for peer in (d_right, d_left, d_y, d_core, d_chip):
        pl.semaphore_signal(barrier, inc=1, device_id=peer, device_id_type=pl.DeviceIdType.MESH)

    @pl.loop(1, 8)
    def _(d):
        pl.semaphore_signal(
            barrier, inc=1, device_id=at(dp, rem(z + d, 8), yh, x), device_id_type=pl.DeviceIdType.MESH
        )

    @pl.when(jnp.logical_not(at_home))
    def _():
        pl.semaphore_signal(barrier, inc=1, device_id=d_p, device_id_type=pl.DeviceIdType.MESH)
        pl.semaphore_wait(barrier, 13)

    @pl.when(at_home)
    def _():
        pl.semaphore_wait(barrier, 12)

    def p_copy(a):
        return remote((tok, dlt)[a], XT.at[a, x, zq, yh], p_s.at[a], p_r.at[a], d_p)

    def p_recv(a):
        mine = XT.at[a, x, z, yh]
        return remote(mine, mine, p_s.at[a], p_r.at[a], d_p)

    def y_copy(a):
        mine = XT.at[a, x, z, yh]
        return remote(mine, mine, y_s.at[a], y_r.at[a], d_y)

    def y_recv(a):
        got = XT.at[a, x, z, 1 - yh]
        return remote(got, got, y_s.at[a], y_r.at[a], d_y)

    def z_copy(a, d):
        mine = XT.at[a, x, z]
        return remote(mine, mine, z_s.at[a, d], z_r.at[a, d], at(dp, rem(z + d, 8), yh, x))

    def z_recv(a, d):
        got = XT.at[a, x, rem(z + 8 - d, 8)]
        return remote(got, got, z_s.at[a, d], z_r.at[a, d], d_y)

    def x_copy(a, k, to_right):
        mine = XT.at[a, x, rem(z + 8 - k, 8)]
        if to_right:
            return remote(mine, mine, xr_s.at[a, k], xr_r.at[a, k], d_right)
        return remote(mine, mine, xl_s.at[a, k], xl_r.at[a, k], d_left)

    def x_recv(a, k, from_left):
        got = XT.at[a, left if from_left else right, rem(z + 8 - k, 8)]
        if from_left:
            return remote(got, got, xr_s.at[a, k], xr_r.at[a, k], d_right)
        return remote(got, got, xl_s.at[a, k], xl_r.at[a, k], d_left)

    def f_copy(a, k, to_right):
        got = XT.at[a, left if to_right else right, rem(z + 8 - k, 8)]
        return remote(got, got, f_s.at[a, k], f_r.at[a, k], d_right if to_right else d_left)

    def f_recv(a, k):
        got = XT.at[a, far, rem(z + 8 - k, 8)]
        return remote(got, got, f_s.at[a, k], f_r.at[a, k], d_right)

    def gather_p(a):
        @pl.when(at_home)
        def _():
            XT[a, x, z, yh] = (tok, dlt)[a][...]

        @pl.when(jnp.logical_not(at_home))
        def _():
            p_copy(a).start()

    def gather_y(a):
        @pl.when(jnp.logical_not(at_home))
        def _():
            p_recv(a).wait_recv()

        y_copy(a).start()

    def gather_z(a):
        y_recv(a).wait_recv()

        @pl.loop(1, 8)
        def _(d):
            z_copy(a, d).start()

    def forward(a, j):
        x_recv(a, 2 * j, True).wait_recv()
        f_copy(a, 2 * j, True).start()
        x_recv(a, 2 * j + 1, False).wait_recv()
        f_copy(a, 2 * j + 1, False).start()

    def gather_x(a, eager):
        @pl.loop(0, 4)
        def _(j):
            @pl.when(j > 0)
            def _():
                z_recv(a, 2 * j).wait_recv()

            x_copy(a, 2 * j, True).start()
            x_copy(a, 2 * j, False).start()
            z_recv(a, 2 * j + 1).wait_recv()
            x_copy(a, 2 * j + 1, True).start()
            x_copy(a, 2 * j + 1, False).start()
            if eager:
                @pl.when(j > 0)
                def _():
                    forward(a, j - 1)

    def gather_end(a):
        @pl.loop(0, 4)
        def _(j):
            x_recv(a, 2 * j, False).wait_recv()
            x_recv(a, 2 * j + 1, True).wait_recv()
            f_recv(a, 2 * j).wait_recv()
            f_recv(a, 2 * j + 1).wait_recv()

    def gather_drain(a):
        @pl.when(jnp.logical_not(at_home))
        def _():
            p_copy(a).wait_send()

        y_copy(a).wait_send()

        @pl.loop(1, 8)
        def _(d):
            z_copy(a, d).wait_send()

        @pl.loop(0, 4)
        def _(j):
            for k in (2 * j, 2 * j + 1):
                x_copy(a, k, True).wait_send()
                x_copy(a, k, False).wait_send()
            f_copy(a, 2 * j, True).wait_send()
            f_copy(a, 2 * j + 1, False).wait_send()

    def o_copy(a, p, to_right):
        return remote(
            PO.at[a, far, p], RXO.at[a, p], o_s.at[a, p], o_r.at[a, p], d_right if to_right else d_left
        )

    def w_copy(a, p, to_right):
        return remote(
            PO.at[a, right if to_right else left, p],
            RXR.at[a, p], w_s.at[a, p], w_r.at[a, p], d_right if to_right else d_left,
        )

    def c_copy(a, p, to_right):
        return remote(
            PO.at[a, right if to_right else left, p],
            RXC.at[a, p], c_s.at[a, p], c_r.at[a, p], d_right if to_right else d_left,
        )

    def zz_copy(a, p):
        return remote(PO.at[a, x, p], ZR.at[a, z], zz_s.at[a, p], zz_r.at[a, z], at(dp, p, yh, x))

    def zz_recv(a, s):
        return remote(ZR.at[a, s], ZR.at[a, s], zz_s.at[a, s], zz_r.at[a, s], d_y)

    def yy_copy(a):
        return remote(YS.at[a, 1 - yh], YR.at[a], yy_s.at[a], yy_r.at[a], d_y)

    def pp_copy(a):
        return remote(FS.at[a], FR.at[a], pp_s.at[a], pp_r.at[a], d_p)

    def sum_start(a):
        @pl.loop(0, 4)
        def _(q):
            o_copy(a, q, True).start()
            o_copy(a, q + 4, False).start()

        @pl.loop(0, 4)
        def _(q):
            w_copy(a, q + 4, True).start()
            w_copy(a, q, False).start()

    def sum_combine(a):
        @pl.loop(0, 4)
        def _(q):
            for p, to_right in ((q, True), (q + 4, False)):
                o_copy(a, p, to_right).wait_recv()
                to = right if to_right else left
                PO[a, to, p] = (PO[a, to, p].astype(F32) + RXO[a, p].astype(F32)).astype(BF16)
                c_copy(a, p, to_right).start()

    def sum_finish(a):
        @pl.loop(0, 4)
        def _(q):
            for p, to_right in ((q, True), (q + 4, False)):
                w_copy(a, p, to_right).wait_recv()
                c_copy(a, p, to_right).wait_recv()
                PO[a, x, p] = (
                    PO[a, x, p].astype(F32) + RXR[a, p].astype(F32) + RXC[a, p].astype(F32)
                ).astype(BF16)

                @pl.when(p != z)
                def _():
                    zz_copy(a, p).start()

    def sum_z(a):
        @pl.loop(1, 8)
        def _(d):
            zz_recv(a, rem(z + d, 8)).wait_recv()

        ZR[a, z] = PO[a, x, z]
        for half in range(2):
            total = ZR[a, 0, half].astype(F32)
            for s in range(1, 8):
                total = total + ZR[a, s, half].astype(F32)
            YS[a, half] = total.astype(BF16)
        yy_copy(a).start()

    def sum_y(a):
        yy_copy(a).wait_recv()
        FS[a] = (YS[a, yh].astype(F32) + YR[a].astype(F32)).astype(BF16)

        @pl.when(jnp.logical_not(at_home))
        def _():
            pp_copy(a).start()

    def sum_p(a):
        out = (bo, gi)[a]

        @pl.when(at_home)
        def _():
            out[...] = FS[a]

        @pl.when(jnp.logical_not(at_home))
        def _():
            pp_copy(a).wait_recv()
            out[...] = FR[a]

    def sum_drain(a):
        @pl.loop(0, 4)
        def _(q):
            for p, to_right in ((q, True), (q + 4, False)):
                o_copy(a, p, to_right).wait_send()
                w_copy(a, p, not to_right).wait_send()
                c_copy(a, p, to_right).wait_send()

        @pl.loop(1, 8)
        def _(d):
            zz_copy(a, rem(z + d, 8)).wait_send()

        yy_copy(a).wait_send()

        @pl.when(jnp.logical_not(at_home))
        def _():
            pp_copy(a).wait_send()

    def columns(a, tb):
        return jnp.concatenate(
            [XT[a, xx, 2 * tb + zb, yy] for zb in range(2) for yy in range(2) for xx in range(4)], axis=0
        )

    def scatter_rows(a, tb, total):
        rounded = total.astype(BF16)
        for zb in range(2):
            for yy in range(2):
                for xx in range(4):
                    jb = zb * 8 + yy * 4 + xx
                    PO[a, xx, 2 * tb + zb, yy] = rounded[jb * FB : (jb + 1) * FB]

    def dot(a, b):
        return jnp.dot(a, b, preferred_element_type=F32)

    def weights(w):
        loads[w].wait()
        WB[w] = MW[w].astype(BF16)

        @pl.loop(0, DS // 128)
        def _(n):
            cols = pl.ds(pl.multiple_of(n * 128, 128), 128)
            WT[w, cols, :] = MW[w, :, cols].T.astype(BF16)

    def core_copy(n, src, dst):
        return remote(src, dst, d_s.at[n], d_r.at[n], d_core)

    def chip_copy(n, src, dst):
        return remote(src, dst, e_s.at[n], e_r.at[n], d_chip)

    def grad(left_op, a):
        GR[...] = jnp.zeros((HID, DS), F32)

        @pl.loop(0, 4)
        def _(tb):
            GR[...] += lax.dot_general(
                left_op[tb], columns(a, tb), (((1,), (1,)), ((), ())), preferred_element_type=F32
            )

    def adamw(w, UO, out):
        loads[3 + w].wait()
        loads[6 + w].wait()

        @pl.loop(0, FFS // 8)
        def _(n):
            rows = pl.ds(pl.multiple_of(n * 8, 8), 8)
            gradient = GR[rows, :]
            moment = beta_first * MOM[w, rows, :] + (1.0 - beta_first) * gradient
            second = beta_second * SEC[w, rows, :] + (1.0 - beta_second) * gradient * gradient
            GR[rows, :] = (moment / correct_first) / (
                jnp.sqrt(second / correct_second) + adam_epsilon
            ) + weight_decay * MW[w, rows, :]

        UO[...] = GR[0:FFS, :].astype(BF16)
        store = pltpu.make_async_copy(UO, out, lsem.at[9 + w])
        store.start()
        return store

    gather_p(0)
    gather_p(1)
    weights(0)
    gather_y(0)
    gather_y(1)
    gather_z(0)
    weights(1)
    gather_x(0, True)
    gather_z(1)
    forward(0, 3)
    weights(2)
    gather_end(0)
    gather_x(1, False)

    @pl.loop(0, 2)
    def _(k):
        cols = columns(0, 2 * (1 - core) + k)
        SD[k, 0] = dot(WB[0], cols)[:PAD].astype(BF16)
        SD[k, 1] = dot(WB[1], cols)[:PAD].astype(BF16)

    core_copy(0, SD, RD).start()

    @pl.loop(0, 2)
    def _(k):
        cols = columns(0, 2 * core + k)
        GUO[k, 0] = dot(WB[0], cols)[:PAD]
        GUO[k, 1] = dot(WB[1], cols)[:PAD]

    core_copy(0, SD, RD).wait_recv()

    @pl.loop(0, 2)
    def _(k):
        GUO[k] = GUO[k] + RD[k].astype(F32)
        SY[k] = GUO[k].astype(BF16)
        chip_copy(k, SY.at[k], RY.at[k]).start()

    @pl.loop(0, 4)
    def _(j):
        forward(1, j)

    @pl.loop(0, 2)
    def _(k):
        chip_copy(k, SY.at[k], RY.at[k]).wait_recv()
        gate_in = GUO[k, 0] + RY[k, 0].astype(F32)
        up_in = GUO[k, 1] + RY[k, 1].astype(F32)
        sig = jax.nn.sigmoid(gate_in)
        active = gate_in * sig
        ACT[k] = active
        US[k] = up_in * (sig * (1.0 + gate_in * (1.0 - sig)))
        mine = HD.at[2 * core + k]
        HD[2 * core + k, 0:PAD, :] = (active * up_in).astype(BF16)
        core_copy(1 + k, mine, mine).start()

    @pl.loop(0, 2)
    def _(k):
        theirs = HD.at[2 * (1 - core) + k]
        core_copy(1 + k, theirs, theirs).wait_recv()

    @pl.loop(0, 4)
    def _(tb):
        scatter_rows(0, tb, dot(WT[2], HD[tb]))

    sum_start(0)
    gather_end(1)

    @pl.loop(0, 2)
    def _(k):
        SD2[k] = dot(WB[2], columns(1, 2 * (1 - core) + k))[:PAD].astype(BF16)

    core_copy(3, SD2, RD2).start()

    @pl.loop(0, 2)
    def _(k):
        DHO[k] = dot(WB[2], columns(1, 2 * core + k))[:PAD]

    core_copy(3, SD2, RD2).wait_recv()

    @pl.loop(0, 2)
    def _(k):
        DHO[k] = DHO[k] + RD2[k].astype(F32)
        SY2[k] = DHO[k].astype(BF16)
        chip_copy(2 + k, SY2.at[k], RY2.at[k]).start()

    sum_combine(0)

    @pl.loop(0, 2)
    def _(k):
        chip_copy(2 + k, SY2.at[k], RY2.at[k]).wait_recv()
        d_hidden = DHO[k] + RY2[k].astype(F32)
        gate, up = DG.at[2 * core + k], DU.at[2 * core + k]
        DG[2 * core + k, 0:PAD, :] = (d_hidden * US[k]).astype(BF16)
        DU[2 * core + k, 0:PAD, :] = (d_hidden * ACT[k]).astype(BF16)
        core_copy(4 + k, gate, gate).start()
        core_copy(6 + k, up, up).start()

    @pl.loop(0, 2)
    def _(k):
        gate, up = DG.at[2 * (1 - core) + k], DU.at[2 * (1 - core) + k]
        core_copy(4 + k, gate, gate).wait_recv()
        core_copy(6 + k, up, up).wait_recv()

    @pl.loop(0, 4)
    def _(tb):
        scatter_rows(1, tb, dot(WT[0], DG[tb]) + dot(WT[1], DU[tb]))

    sum_start(1)
    sum_finish(0)
    grad(HD, 1)
    store_down = adamw(2, UO2, ud)
    sum_combine(1)
    sum_z(0)
    grad(DG, 0)
    store_gate = adamw(0, UO0, ug)
    sum_y(0)
    grad(DU, 0)
    store_up = adamw(1, UO1, uu)
    sum_finish(1)
    sum_p(0)
    sum_z(1)
    gather_drain(0)
    gather_drain(1)
    sum_drain(0)
    core_copy(0, SD, RD).wait_send()
    core_copy(3, SD2, RD2).wait_send()

    @pl.loop(0, 2)
    def _(k):
        hid, gate, up = HD.at[2 * core + k], DG.at[2 * core + k], DU.at[2 * core + k]
        chip_copy(k, SY.at[k], RY.at[k]).wait_send()
        chip_copy(2 + k, SY2.at[k], RY2.at[k]).wait_send()
        core_copy(1 + k, hid, hid).wait_send()
        core_copy(4 + k, gate, gate).wait_send()
        core_copy(6 + k, up, up).wait_send()

    sum_y(1)
    sum_p(1)
    sum_drain(1)
    store_down.wait()
    store_gate.wait()
    store_up.wait()


def step(tok, dlt, states):
    def vmem(*shape, dtype=BF16):
        return pltpu.VMEM(shape, dtype)

    dma = pltpu.SemaphoreType.DMA
    out = jax.ShapeDtypeStruct
    shard, update = out((FB, TB), BF16), out((FFS, DS), BF16)
    in_vmem = pl.BlockSpec(memory_space=pltpu.VMEM)
    in_any = pl.BlockSpec(memory_space=pl.ANY)
    scratch = [
        vmem(2, 4, 8, 2, FB, TB),
        vmem(2, 4, 8, 2, FB, TB),
        vmem(2, 8, 2, FB, TB),
        vmem(2, 8, 2, FB, TB),
        vmem(2, 8, 2, FB, TB),
        vmem(2, 8, 2, FB, TB),
        vmem(2, 2, FB, TB),
        vmem(2, FB, TB),
        vmem(2, FB, TB),
        vmem(2, FB, TB),
        vmem(3, HID, DS, dtype=F32),
        vmem(3, FFS, DS, dtype=F32),
        vmem(3, FFS, DS, dtype=F32),
        vmem(3, HID, DS),
        vmem(3, DS, HID),
        vmem(4, HID, TB),
        vmem(4, HID, TB),
        vmem(4, HID, TB),
        vmem(2, 2, PAD, TB, dtype=F32),
        vmem(2, PAD, TB, dtype=F32),
        vmem(2, PAD, TB, dtype=F32),
        vmem(2, PAD, TB, dtype=F32),
        vmem(2, 2, PAD, TB),
        vmem(2, 2, PAD, TB),
        vmem(2, 2, PAD, TB),
        vmem(2, 2, PAD, TB),
        vmem(2, PAD, TB),
        vmem(2, PAD, TB),
        vmem(2, PAD, TB),
        vmem(2, PAD, TB),
        vmem(HID, DS, dtype=F32),
        vmem(FFS, DS),
        vmem(FFS, DS),
        vmem(FFS, DS),
        dma((12,)),
        dma((2,)), dma((2,)),
        dma((2,)), dma((2,)),
        dma((2, 8)), dma((2, 8)),
        dma((2, 8)), dma((2, 8)),
        dma((2, 8)), dma((2, 8)),
        dma((2, 8)), dma((2, 8)),
        dma((2, 8)), dma((2, 8)),
        dma((2, 8)), dma((2, 8)),
        dma((2, 8)), dma((2, 8)),
        dma((2, 8)), dma((2, 8)),
        dma((2,)), dma((2,)),
        dma((2,)), dma((2,)),
        dma((8,)), dma((8,)),
        dma((4,)), dma((4,)),
    ]
    return pl.pallas_call(
        kernel,
        out_shape=[shard, shard, update, update, update],
        in_specs=[in_vmem] * 2 + [in_any] * 9,
        out_specs=[in_vmem] * 2 + [in_any] * 3,
        scratch_shapes=scratch,
        compiler_params=pltpu.CompilerParams(
            collective_id=0, has_side_effects=True, vmem_limit_bytes=58 * 1024 * 1024
        ),
        cost_estimate=pl.CostEstimate(flops=5_100_000_000, bytes_accessed=12_000_000, transcendentals=1_000_000),
        name="fused_step",
    )(tok, dlt, *states)


def body(tokens, cotangent, pass_counts, group_ids, token_rollout, *states):
    reward = pass_counts.astype(F32) / TESTS
    same_group = (group_ids[:, None] == group_ids[None, :]).astype(F32)
    baseline = jnp.sum(same_group * reward[None, :], axis=1) / jnp.sum(same_group, axis=1)
    advantage = reward - baseline
    picker = (token_rollout[:, None] == jnp.arange(ROLL, dtype=jnp.int32)[None, :]).astype(F32)
    token_adv = jnp.sum(picker * advantage[None, :], axis=1)
    delta = (-token_adv[:, None] * cotangent.astype(F32)).astype(BF16)
    block_out, grad_input, update_gate, update_up, update_down = step(tokens.T, delta.T, states)
    return block_out.T, grad_input.T, update_gate, update_up, update_down


def solution(mesh):
    act, rep, weight = P("dp", "fsdp"), P(), P("fsdp", "dp")
    return jax.shard_map(
        body,
        mesh=mesh,
        in_specs=(act, act, rep, rep, P("dp")) + (weight,) * 9,
        out_specs=(act, act, weight, weight, weight),
        check_vma=False,
    )
```

```python
import jax
import jax.numpy as jnp
from jax import lax
from jax.experimental import pallas as pl
from jax.experimental.pallas import tpu as pltpu
from jax.sharding import PartitionSpec as P

ROLL = 64
TESTS = 8
beta_first = 0.9
beta_second = 0.95
adam_epsilon = 1e-08
weight_decay = 0.1
correct_first = 1.0 - 0.9**10
correct_second = 1.0 - 0.95**10

FFS = 216
PAD = 224
HID = 256
DS = 1280
FB = 80
TB = 256
F32 = jnp.float32
BF16 = jnp.bfloat16


def rem(a, b):
    return lax.rem(a, jnp.int32(b))


def div(a, b):
    return lax.div(a, jnp.int32(b))


def remote(src, dst, send, recv, device):
    return pltpu.make_async_remote_copy(
        src_ref=src,
        dst_ref=dst,
        send_sem=send,
        recv_sem=recv,
        device_id=device,
        device_id_type=pl.DeviceIdType.MESH,
    )


def kernel(
    tok, cot, counts, groups, rolls, mg, mu, md, og, ou, od, sg, su, sd,
    bo, gi, ug, uu, ud,
    TT, XT, PO, RV, RXO, RXR, RXC, ZR, YS, FR,
    MW, MOM, SEC, WB, WT, HD, DG, DU, GUO, ACT, US, DHO,
    SD, RD, SY, RY, SD2, RD2, SY2, RY2, GR, UO0, UO1, UO2,
    lsem, z_s, z_r, xr_s, xr_r, xl_s, xl_r, f_s, f_r,
    v_s, v_r, u_s, u_r, o_s, o_r, w_s, w_r, c_s, c_r, zz_s, zz_r, q_s, q_r,
    d_s, d_r, e_s, e_r,
):
    dp = lax.axis_index("dp")
    fs = lax.axis_index("fsdp")
    z, yh, x = div(fs, 8), rem(div(fs, 4), 2), rem(fs, 4)
    core = rem(dp, 2)
    right, left, far = rem(x + 1, 4), rem(x + 3, 4), rem(x + 2, 4)

    def at(dp_, z_, y_, x_):
        return (dp_, z_ * 8 + y_ * 4 + x_)

    d_right, d_left = at(dp, z, yh, right), at(dp, z, yh, left)
    home = div(z, 2)
    own = 2 * dp + rem(z, 2)
    at_home = home == dp
    d_y = at(dp, z, 1 - yh, x)
    d_core = at(dp + 1 - 2 * core, z, yh, x)
    d_chip = at(rem(dp + 2, 4), z, yh, x)

    srcs = (mg, mu, md, og, ou, od, sg, su, sd)
    loads = []
    for n, src in enumerate(srcs):
        dst = (MW, MOM, SEC)[n // 3].at[n % 3, pl.ds(0, FFS)]
        loads.append(pltpu.make_async_copy(src, dst, lsem.at[n]))
    for load in loads:
        load.start()

    for w in range(3):
        MW[w, FFS:HID, :] = jnp.zeros((HID - FFS, DS), F32)
    for buf in (HD, DG, DU):
        for n in range(4):
            buf[n, PAD:HID, :] = jnp.zeros((HID - PAD, TB), BF16)

    def is_self(n, t):
        return jnp.logical_and(jnp.logical_and(at_home, n == 0), t == yh)

    barrier = pltpu.get_barrier_semaphore()

    def greet(peer):
        pl.semaphore_signal(barrier, inc=1, device_id=peer, device_id_type=pl.DeviceIdType.MESH)

    for peer in (d_right, d_left, d_core, d_chip, d_y):
        greet(peer)

    @pl.loop(1, 8)
    def _(n):
        greet(at(dp, rem(z + n, 8), yh, x))

    @pl.loop(0, 8)
    def _(n):
        for t in range(2):
            @pl.when(jnp.logical_not(is_self(n, t)))
            def _():
                greet(at(div(rem(z + n, 8), 2), 2 * dp + rem(z + n, 2), t, x))

    reward = counts[...].astype(F32) / TESTS
    group = groups[...].astype(F32)
    group_col = jnp.broadcast_to(group, (ROLL, ROLL)).T
    same = (group_col == group).astype(F32)
    baseline = jnp.sum(same * reward, axis=1, keepdims=True) / jnp.sum(same, axis=1, keepdims=True)
    reward_col = jnp.broadcast_to(reward, (ROLL, ROLL)).T[:, 0:1]
    advantage = reward_col - baseline
    rollout = lax.broadcasted_iota(jnp.int32, (ROLL, TB), 0)
    token_adv = jnp.sum(jnp.where(rollout == rolls[...], advantage, 0.0), axis=0, keepdims=True)
    TT[0] = tok[...]
    TT[1] = (-token_adv * cot[...].astype(F32)).astype(BF16)

    @pl.when(at_home)
    def _():
        pl.semaphore_wait(barrier, 27)

    @pl.when(jnp.logical_not(at_home))
    def _():
        pl.semaphore_wait(barrier, 28)

    def z_copy(a, n, t):
        return remote(
            TT.at[a], XT.at[a, x, own, yh], z_s.at[a, n, t], z_r.at[a, n, yh], at(home, rem(own + n, 8), t, x)
        )

    def z_start(a, n):
        for t in range(2):
            @pl.when(jnp.logical_and(jnp.logical_not(is_self(n, t)), jnp.logical_or(n >= 2, t == yh)))
            def _():
                z_copy(a, n, t).start()

    def z_recv(a, k):
        for s in range(2):
            @pl.when(jnp.logical_and(jnp.logical_not(is_self(k, s)), jnp.logical_or(k >= 2, s == yh)))
            def _():
                got = XT.at[a, x, rem(z + 8 - k, 8), s]
                remote(got, got, z_s.at[a, k, s], z_r.at[a, k, s], d_right).wait_recv()

    def piece(a, xx, k):
        block = XT.at[a, xx, rem(z + 8 - k, 8)]
        return block.at[yh] if isinstance(k, int) and k < 2 else block

    def x_copy(a, k, to_right):
        mine = piece(a, x, k)
        if to_right:
            return remote(mine, mine, xr_s.at[a, k], xr_r.at[a, k], d_right)
        return remote(mine, mine, xl_s.at[a, k], xl_r.at[a, k], d_left)

    def x_recv(a, k, from_left):
        got = piece(a, left if from_left else right, k)
        if from_left:
            return remote(got, got, xr_s.at[a, k], xr_r.at[a, k], d_right)
        return remote(got, got, xl_s.at[a, k], xl_r.at[a, k], d_left)

    def f_copy(a, k, to_right):
        got = piece(a, left if to_right else right, k)
        return remote(got, got, f_s.at[a, k], f_r.at[a, k], d_right if to_right else d_left)

    def f_recv(a, k):
        got = piece(a, far, k)
        return remote(got, got, f_s.at[a, k], f_r.at[a, k], d_right)

    def v_copy(a, k, xx):
        mine = XT.at[a, xx, rem(z + 8 - k, 8), yh]
        return remote(mine, mine, v_s.at[a, k, xx], v_r.at[a, k, xx], d_y)

    def v_recv(a, k, xx):
        got = XT.at[a, xx, rem(z + 8 - k, 8), 1 - yh]
        return remote(got, got, v_s.at[a, k, xx], v_r.at[a, k, xx], d_y)

    def gather_home(a):
        @pl.when(at_home)
        def _():
            XT[a, x, own, yh] = TT[a]

    def forward(a, j):
        x_recv(a, 2 * j, True).wait_recv()
        f_copy(a, 2 * j, True).start()
        x_recv(a, 2 * j + 1, False).wait_recv()
        f_copy(a, 2 * j + 1, False).start()

    def forward_first(a):
        forward(a, 0)
        x_recv(a, 0, False).wait_recv()
        x_recv(a, 1, True).wait_recv()

    def v_start(a, *sides):
        for k in range(2):
            for n in sides:
                v_copy(a, k, n).start()

    def forward_far(a):
        for k in range(2):
            f_recv(a, k).wait_recv()

    def gather_step(a, j):
        for k in (2 * j, 2 * j + 1):
            z_recv(a, k)
            x_copy(a, k, True).start()
            x_copy(a, k, False).start()
            if a == 0:
                @pl.when(k < 5)
                def _():
                    z_start(0, k + 3)

                @pl.when(k >= 5)
                def _():
                    z_start(1, k - 5)

    def gather_x(a):
        gather_step(a, 0)
        if a == 0:
            v_start(0, x)
            gather_step(a, 1)
            forward_first(a)
            v_start(0, left, right)

            @pl.loop(2, 4)
            def _(j):
                gather_step(a, j)
                forward(a, j - 1)

            @pl.loop(3, 8)
            def _(n):
                z_start(1, n)
        else:
            @pl.loop(1, 4)
            def _(j):
                gather_step(a, j)

    def gather_end(a):
        @pl.loop(1, 4)
        def _(j):
            x_recv(a, 2 * j, False).wait_recv()
            x_recv(a, 2 * j + 1, True).wait_recv()
            f_recv(a, 2 * j).wait_recv()
            f_recv(a, 2 * j + 1).wait_recv()

        for k in range(2):
            @pl.loop(0, 4)
            def _(n):
                v_recv(a, k, n).wait_recv()

    def gather_drain(a):
        for k in range(8):
            for t in range(2):
                @pl.when(jnp.logical_and(jnp.logical_not(is_self(k, t)), jnp.logical_or(k >= 2, t == yh)))
                def _():
                    z_copy(a, k, t).wait_send()
            x_copy(a, k, True).wait_send()
            x_copy(a, k, False).wait_send()
            f_copy(a, k, k % 2 == 0).wait_send()
        for k in range(2):
            @pl.loop(0, 4)
            def _(n):
                v_copy(a, k, n).wait_send()

    def place(k):
        return rem(z + k, 8)

    def late(k):
        return isinstance(k, int) and k >= 6

    def part(a, xx, k):
        block = PO.at[a, xx, place(k)]
        return block.at[yh] if late(k) else block

    def slot(buf, a, k):
        return buf.at[a, k, 0] if late(k) else buf.at[a, k]

    def u_copy(a, k, n):
        return remote(
            PO.at[a, n, place(k), 1 - yh], RV.at[a, k - 6, n], u_s.at[a, k - 6, n], u_r.at[a, k - 6, n], d_y
        )

    def o_copy(a, k, to_right):
        return remote(
            part(a, far, k), slot(RXO, a, k), o_s.at[a, k], o_r.at[a, k], d_right if to_right else d_left
        )

    def w_copy(a, k, to_right):
        return remote(
            part(a, right if to_right else left, k),
            slot(RXR, a, k), w_s.at[a, k], w_r.at[a, k], d_right if to_right else d_left,
        )

    def c_copy(a, k, to_right):
        return remote(
            part(a, right if to_right else left, k),
            slot(RXC, a, k), c_s.at[a, k], c_r.at[a, k], d_right if to_right else d_left,
        )

    def zz_copy(a, k):
        dst = ZR.at[a, k, yh] if late(k) else ZR.at[a, k]
        return remote(part(a, x, k), dst, zz_s.at[a, k], zz_r.at[a, k], at(dp, place(k), yh, x))

    def q_copy(a, s):
        return remote(YS.at[a, s], FR.at[a, yh], q_s.at[a, s], q_r.at[a, yh], at(home, own, s, x))

    def halves(j):
        return ((2 * j, True), (2 * j + 1, False))

    def o_start(a, j):
        for k, to_right in halves(j):
            o_copy(a, k, to_right).start()

    def w_start(a, j):
        for k, to_right in halves(j):
            w_copy(a, k, not to_right).start()

    def sum_start(a):
        for k in (6, 7):
            @pl.loop(0, 4)
            def _(n):
                u_copy(a, k, n).start()

        o_start(a, 0)
        o_start(a, 1)
        w_start(a, 0)
        if a == 0:
            o_start(a, 2)
            w_start(a, 1)
            w_start(a, 2)

    def fold_y(a):
        for k in (6, 7):
            @pl.loop(0, 4)
            def _(n):
                u_copy(a, k, n).wait_recv()
                mine = PO.at[a, n, place(k), yh]
                mine[...] = (mine[...].astype(F32) + RV[a, k - 6, n].astype(F32)).astype(BF16)

    def combine(a, j):
        for k, to_right in halves(j):
            o_copy(a, k, to_right).wait_recv()
            mine, got = part(a, right if to_right else left, k), slot(RXO, a, k)
            mine[...] = (mine[...].astype(F32) + got[...].astype(F32)).astype(BF16)
            c_copy(a, k, to_right).start()

    def finish(a, j):
        for k, to_right in halves(j):
            w_copy(a, k, not to_right).wait_recv()
            c_copy(a, k, to_right).wait_recv()
            mine = part(a, x, k)
            mine[...] = (
                mine[...].astype(F32) + slot(RXR, a, k)[...].astype(F32) + slot(RXC, a, k)[...].astype(F32)
            ).astype(BF16)
            if late(k):
                zz_copy(a, k).start()
            else:
                @pl.when(k > 0)
                def _():
                    zz_copy(a, k).start()

    def sum_finish(a):
        @pl.loop(0, 3)
        def _(j):
            finish(a, j)

        finish(a, 3)

    def sum_z(a):
        for k in range(1, 8):
            zz_copy(a, k).wait_recv()
        for s in range(2):
            total = PO[a, x, z, s].astype(F32)
            for k in range(1, 6):
                total = total + ZR[a, k, s].astype(F32)

            @pl.when(s == yh)
            def _():
                YS[a, s] = (total + ZR[a, 6, s].astype(F32) + ZR[a, 7, s].astype(F32)).astype(BF16)

            @pl.when(s != yh)
            def _():
                YS[a, s] = total.astype(BF16)

            @pl.when(jnp.logical_not(is_self(0, s)))
            def _():
                q_copy(a, s).start()

    def sum_end(a):
        for s in range(2):
            @pl.when(is_self(0, s))
            def _():
                FR[a, s] = YS[a, s]

            @pl.when(jnp.logical_not(is_self(0, s)))
            def _():
                remote(FR.at[a, s], FR.at[a, s], q_s.at[a, s], q_r.at[a, s], d_right).wait_recv()

        (bo, gi)[a][...] = (FR[a, 0].astype(F32) + FR[a, 1].astype(F32)).astype(BF16)

    def sum_drain(a):
        for k in (6, 7):
            @pl.loop(0, 4)
            def _(n):
                u_copy(a, k, n).wait_send()

        for j in range(4):
            for k, to_right in halves(j):
                o_copy(a, k, to_right).wait_send()
                w_copy(a, k, not to_right).wait_send()
                c_copy(a, k, to_right).wait_send()
                if k > 0:
                    zz_copy(a, k).wait_send()

        for s in range(2):
            @pl.when(jnp.logical_not(is_self(0, s)))
            def _():
                q_copy(a, s).wait_send()

    def columns(a, tb):
        return jnp.concatenate(
            [XT[a, xx, 2 * tb + zb, yy] for zb in range(2) for yy in range(2) for xx in range(4)], axis=0
        )

    def scatter_rows(a, tb, total):
        rounded = total.astype(BF16)
        for zb in range(2):
            for yy in range(2):
                for xx in range(4):
                    jb = zb * 8 + yy * 4 + xx
                    PO[a, xx, 2 * tb + zb, yy] = rounded[jb * FB : (jb + 1) * FB]

    def dot(a, b):
        return jnp.dot(a, b, preferred_element_type=F32)

    def weights(w):
        loads[w].wait()
        WB[w] = MW[w].astype(BF16)

        @pl.loop(0, DS // 128)
        def _(n):
            cols = pl.ds(pl.multiple_of(n * 128, 128), 128)
            WT[w, cols, :] = MW[w, :, cols].T.astype(BF16)

    def core_copy(n, src, dst):
        return remote(src, dst, d_s.at[n], d_r.at[n], d_core)

    def chip_copy(n, src, dst):
        return remote(src, dst, e_s.at[n], e_r.at[n], d_chip)

    def grad(left_op, a):
        GR[...] = jnp.zeros((HID, DS), F32)

        @pl.loop(0, 4)
        def _(tb):
            GR[...] += lax.dot_general(
                left_op[tb], columns(a, tb), (((1,), (1,)), ((), ())), preferred_element_type=F32
            )

    def adamw(w, UO, out):
        loads[3 + w].wait()
        loads[6 + w].wait()

        @pl.loop(0, FFS // 8)
        def _(n):
            rows = pl.ds(pl.multiple_of(n * 8, 8), 8)
            gradient = GR[rows, :]
            moment = beta_first * MOM[w, rows, :] + (1.0 - beta_first) * gradient
            second = beta_second * SEC[w, rows, :] + (1.0 - beta_second) * gradient * gradient
            GR[rows, :] = (moment / correct_first) / (
                jnp.sqrt(second / correct_second) + adam_epsilon
            ) + weight_decay * MW[w, rows, :]

        UO[...] = GR[0:FFS, :].astype(BF16)
        store = pltpu.make_async_copy(UO, out, lsem.at[9 + w])
        store.start()
        return store

    gather_home(0)

    @pl.loop(0, 3)
    def _(n):
        z_start(0, n)

    gather_home(1)
    weights(0)
    weights(1)
    gather_x(0)
    forward_far(0)
    v_start(0, far)
    forward(0, 3)
    weights(2)
    gather_x(1)
    gather_end(0)

    @pl.loop(0, 2)
    def _(k):
        cols = columns(0, 2 * (1 - core) + k)
        SD[k, 0] = dot(WB[0], cols)[:PAD].astype(BF16)
        SD[k, 1] = dot(WB[1], cols)[:PAD].astype(BF16)
        core_copy(8 * k, SD.at[k], RD.at[k]).start()

    @pl.loop(0, 2)
    def _(k):
        cols = columns(0, 2 * core + k)
        core_copy(8 * k, SD.at[k], RD.at[k]).wait_recv()
        gate = dot(WB[0], cols)[:PAD] + RD[k, 0].astype(F32)
        up = dot(WB[1], cols)[:PAD] + RD[k, 1].astype(F32)
        GUO[k, 0] = gate
        GUO[k, 1] = up
        SY[k, 0] = gate.astype(BF16)
        SY[k, 1] = up.astype(BF16)
        chip_copy(k, SY.at[k], RY.at[k]).start()

    forward_first(1)

    @pl.loop(1, 4)
    def _(j):
        forward(1, j)

    @pl.loop(0, 2)
    def _(k):
        chip_copy(k, SY.at[k], RY.at[k]).wait_recv()
        gate_in = GUO[k, 0] + RY[k, 0].astype(F32)
        up_in = GUO[k, 1] + RY[k, 1].astype(F32)
        sig = jax.nn.sigmoid(gate_in)
        active = gate_in * sig
        ACT[k] = active
        US[k] = up_in * (sig * (1.0 + gate_in * (1.0 - sig)))
        mine = HD.at[2 * core + k]
        HD[2 * core + k, 0:PAD, :] = (active * up_in).astype(BF16)
        core_copy(1 + k, mine, mine).start()

    forward_far(1)
    v_start(1, x, left, right, far)

    @pl.loop(0, 2)
    def _(k):
        theirs = HD.at[2 * (1 - core) + k]
        core_copy(1 + k, theirs, theirs).wait_recv()

    @pl.loop(0, 4)
    def _(tb):
        scatter_rows(0, tb, dot(WT[2], HD[tb]))

    sum_start(0)
    gather_end(1)

    @pl.loop(0, 2)
    def _(k):
        SD2[k] = dot(WB[2], columns(1, 2 * (1 - core) + k))[:PAD].astype(BF16)

    core_copy(3, SD2, RD2).start()

    @pl.loop(0, 2)
    def _(k):
        DHO[k] = dot(WB[2], columns(1, 2 * core + k))[:PAD]

    core_copy(3, SD2, RD2).wait_recv()

    @pl.loop(0, 2)
    def _(k):
        DHO[k] = DHO[k] + RD2[k].astype(F32)
        SY2[k] = DHO[k].astype(BF16)
        chip_copy(2 + k, SY2.at[k], RY2.at[k]).start()

    combine(0, 0)
    fold_y(0)
    o_start(0, 3)
    w_start(0, 3)
    for j in range(1, 4):
        combine(0, j)
    grad(HD, 1)
    store_down = adamw(2, UO2, ud)

    @pl.loop(0, 2)
    def _(k):
        chip_copy(2 + k, SY2.at[k], RY2.at[k]).wait_recv()
        d_hidden = DHO[k] + RY2[k].astype(F32)
        gate, up = DG.at[2 * core + k], DU.at[2 * core + k]
        DG[2 * core + k, 0:PAD, :] = (d_hidden * US[k]).astype(BF16)
        DU[2 * core + k, 0:PAD, :] = (d_hidden * ACT[k]).astype(BF16)
        core_copy(4 + k, gate, gate).start()
        core_copy(6 + k, up, up).start()

    @pl.loop(0, 2)
    def _(k):
        gate, up = DG.at[2 * (1 - core) + k], DU.at[2 * (1 - core) + k]
        core_copy(4 + k, gate, gate).wait_recv()
        core_copy(6 + k, up, up).wait_recv()

    @pl.loop(0, 4)
    def _(tb):
        scatter_rows(1, tb, dot(WT[0], DG[tb]) + dot(WT[1], DU[tb]))

    sum_start(1)
    sum_finish(0)
    combine(1, 0)
    o_start(1, 2)
    w_start(1, 1)
    grad(DG, 0)
    store_gate = adamw(0, UO0, ug)
    fold_y(1)
    combine(1, 1)
    o_start(1, 3)
    w_start(1, 2)
    finish(1, 0)
    sum_z(0)
    combine(1, 2)
    w_start(1, 3)
    finish(1, 1)
    grad(DU, 0)
    store_up = adamw(1, UO1, uu)
    combine(1, 3)
    finish(1, 2)
    finish(1, 3)
    sum_end(0)
    sum_z(1)
    gather_drain(0)
    gather_drain(1)
    sum_drain(0)
    for k in range(2):
        core_copy(8 * k, SD.at[k], RD.at[k]).wait_send()
    core_copy(3, SD2, RD2).wait_send()

    @pl.loop(0, 2)
    def _(k):
        hid, gate, up = HD.at[2 * core + k], DG.at[2 * core + k], DU.at[2 * core + k]
        chip_copy(k, SY.at[k], RY.at[k]).wait_send()
        chip_copy(2 + k, SY2.at[k], RY2.at[k]).wait_send()
        core_copy(1 + k, hid, hid).wait_send()
        core_copy(4 + k, gate, gate).wait_send()
        core_copy(6 + k, up, up).wait_send()

    sum_end(1)
    sum_drain(1)
    store_down.wait()
    store_gate.wait()
    store_up.wait()


def step(*inputs):
    def vmem(*shape, dtype=BF16):
        return pltpu.VMEM(shape, dtype)

    dma = pltpu.SemaphoreType.DMA
    out = jax.ShapeDtypeStruct
    shard, update = out((FB, TB), BF16), out((FFS, DS), BF16)
    in_vmem = pl.BlockSpec(memory_space=pltpu.VMEM)
    in_any = pl.BlockSpec(memory_space=pl.ANY)
    scratch = [
        vmem(2, FB, TB),
        vmem(2, 4, 8, 2, FB, TB),
        vmem(2, 4, 8, 2, FB, TB),
        vmem(2, 2, 4, FB, TB),
        vmem(2, 8, 2, FB, TB),
        vmem(2, 8, 2, FB, TB),
        vmem(2, 8, 2, FB, TB),
        vmem(2, 8, 2, FB, TB),
        vmem(2, 2, FB, TB),
        vmem(2, 2, FB, TB),
        vmem(3, HID, DS, dtype=F32),
        vmem(3, FFS, DS, dtype=F32),
        vmem(3, FFS, DS, dtype=F32),
        vmem(3, HID, DS),
        vmem(3, DS, HID),
        vmem(4, HID, TB),
        vmem(4, HID, TB),
        vmem(4, HID, TB),
        vmem(2, 2, PAD, TB, dtype=F32),
        vmem(2, PAD, TB, dtype=F32),
        vmem(2, PAD, TB, dtype=F32),
        vmem(2, PAD, TB, dtype=F32),
        vmem(2, 2, PAD, TB),
        vmem(2, 2, PAD, TB),
        vmem(2, 2, PAD, TB),
        vmem(2, 2, PAD, TB),
        vmem(2, PAD, TB),
        vmem(2, PAD, TB),
        vmem(2, PAD, TB),
        vmem(2, PAD, TB),
        vmem(HID, DS, dtype=F32),
        vmem(FFS, DS),
        vmem(FFS, DS),
        vmem(FFS, DS),
        dma((12,)),
        dma((2, 8, 2)), dma((2, 8, 2)),
        dma((2, 8)), dma((2, 8)),
        dma((2, 8)), dma((2, 8)),
        dma((2, 8)), dma((2, 8)),
        dma((2, 2, 4)), dma((2, 2, 4)),
        dma((2, 2, 4)), dma((2, 2, 4)),
        dma((2, 8)), dma((2, 8)),
        dma((2, 8)), dma((2, 8)),
        dma((2, 8)), dma((2, 8)),
        dma((2, 8)), dma((2, 8)),
        dma((2, 2)), dma((2, 2)),
        dma((9,)), dma((9,)),
        dma((4,)), dma((4,)),
    ]
    return pl.pallas_call(
        kernel,
        out_shape=[shard, shard, update, update, update],
        in_specs=[in_vmem] * 5 + [in_any] * 9,
        out_specs=[in_vmem] * 2 + [in_any] * 3,
        scratch_shapes=scratch,
        compiler_params=pltpu.CompilerParams(
            collective_id=0, has_side_effects=True, vmem_limit_bytes=58 * 1024 * 1024
        ),
        cost_estimate=pl.CostEstimate(flops=5_100_000_000, bytes_accessed=12_000_000, transcendentals=1_000_000),
        name="fused_step",
    )(*inputs)


def handing_on(*refs):
    for a, b in zip(refs[:5], refs[5:]):
        b[...] = a[...]


def hand_on(*results):
    in_vmem = pl.BlockSpec(memory_space=pltpu.VMEM)
    return pl.pallas_call(
        handing_on,
        out_shape=[jax.ShapeDtypeStruct(r.shape, r.dtype) for r in results],
        in_specs=[in_vmem] * 5,
        out_specs=[in_vmem] * 5,
        name="hand_on",
    )(*results)


def body(tokens, cotangent, pass_counts, group_ids, token_rollout, *states):
    results = step(
        tokens.T,
        cotangent.T,
        pass_counts.reshape(1, ROLL),
        group_ids.reshape(1, ROLL),
        token_rollout.reshape(1, TB),
        *states,
    )
    block_out, grad_input, update_gate, update_up, update_down = hand_on(*results)
    return block_out.T, grad_input.T, update_gate, update_up, update_down


def solution(mesh):
    act, rep, weight = P("dp", "fsdp"), P(), P("fsdp", "dp")
    return jax.shard_map(
        body,
        mesh=mesh,
        in_specs=(act, act, rep, rep, P("dp")) + (weight,) * 9,
        out_specs=(act, act, weight, weight, weight),
        check_vma=False,
    )
```

```python
import jax
import jax.numpy as jnp
from jax import lax
from jax.experimental import pallas as pl
from jax.experimental.pallas import tpu as pltpu
from jax.sharding import PartitionSpec as P

ROLL = 64
TESTS = 8
beta_first = 0.9
beta_second = 0.95
adam_epsilon = 1e-08
weight_decay = 0.1
correct_first = 1.0 - 0.9**10
correct_second = 1.0 - 0.95**10

FFS = 216
PAD = 224
HID = 256
DS = 1280
FB = 80
TB = 256
NEAR = (0, 1, 7, 2, 6, 3, 5, 4)
FAR = (4, 3, 5, 2, 6, 1, 7, 0)
F32 = jnp.float32
BF16 = jnp.bfloat16


def rem(a, b):
    return lax.rem(a, jnp.int32(b))


def div(a, b):
    return lax.div(a, jnp.int32(b))


def remote(src, dst, send, recv, device):
    return pltpu.make_async_remote_copy(
        src_ref=src,
        dst_ref=dst,
        send_sem=send,
        recv_sem=recv,
        device_id=device,
        device_id_type=pl.DeviceIdType.MESH,
    )


def kernel(
    tok, cot, counts, groups, rolls, mg, mu, md, og, ou, od, sg, su, sd,
    bo, gi, ug, uu, ud,
    TT, XT, PO, RV, RXO, RXR, RXC, ZR, YS, FR,
    MW, MOM, SEC, WB, WT, HD, DG, DU, GUO, ACT, US, DHO,
    SD, RD, SY, RY, SD2, RD2, SY2, RY2, GR, UO0, UO1, UO2,
    lsem, z_s, z_r, xr_s, xr_r, xl_s, xl_r, f_s, f_r,
    v_s, v_r, u_s, u_r, o_s, o_r, w_s, w_r, c_s, c_r, zz_s, zz_r, q_s, q_r,
    d_s, d_r, e_s, e_r,
):
    dp = lax.axis_index("dp")
    fs = lax.axis_index("fsdp")
    z, yh, x = div(fs, 8), rem(div(fs, 4), 2), rem(fs, 4)
    core = rem(dp, 2)
    right, left, far = rem(x + 1, 4), rem(x + 3, 4), rem(x + 2, 4)

    def at(dp_, z_, y_, x_):
        return (dp_, z_ * 8 + y_ * 4 + x_)

    d_right, d_left = at(dp, z, yh, right), at(dp, z, yh, left)
    home = div(z, 2)
    own = 2 * dp + rem(z, 2)
    at_home = home == dp
    d_y = at(dp, z, 1 - yh, x)
    d_core = at(dp + 1 - 2 * core, z, yh, x)
    d_chip = at(rem(dp + 2, 4), z, yh, x)

    srcs = (mg, mu, md, og, ou, od, sg, su, sd)
    loads = []
    for n, src in enumerate(srcs):
        dst = (MW, MOM, SEC)[n // 3].at[n % 3, pl.ds(0, FFS)]
        loads.append(pltpu.make_async_copy(src, dst, lsem.at[n]))
    for load in loads:
        load.start()

    for w in range(3):
        MW[w, FFS:HID, :] = jnp.zeros((HID - FFS, DS), F32)
    for buf in (HD, DG, DU):
        for n in range(4):
            buf[n, PAD:HID, :] = jnp.zeros((HID - PAD, TB), BF16)

    def is_self(n, t):
        return jnp.logical_and(jnp.logical_and(at_home, n == 0), t == yh)

    barrier = pltpu.get_barrier_semaphore()

    def greet(peer):
        pl.semaphore_signal(barrier, inc=1, device_id=peer, device_id_type=pl.DeviceIdType.MESH)

    for peer in (d_right, d_left, d_core, d_chip, d_y):
        greet(peer)

    @pl.loop(1, 8)
    def _(n):
        greet(at(dp, rem(z + n, 8), yh, x))

    @pl.loop(0, 8)
    def _(n):
        for t in range(2):
            @pl.when(jnp.logical_not(is_self(n, t)))
            def _():
                greet(at(div(rem(z + n, 8), 2), 2 * dp + rem(z + n, 2), t, x))

    reward = counts[...].astype(F32) / TESTS
    group = groups[...].astype(F32)
    group_col = jnp.broadcast_to(group, (ROLL, ROLL)).T
    same = (group_col == group).astype(F32)
    baseline = jnp.sum(same * reward, axis=1, keepdims=True) / jnp.sum(same, axis=1, keepdims=True)
    reward_col = jnp.broadcast_to(reward, (ROLL, ROLL)).T[:, 0:1]
    advantage = reward_col - baseline
    rollout = lax.broadcasted_iota(jnp.int32, (ROLL, TB), 0)
    token_adv = jnp.sum(jnp.where(rollout == rolls[...], advantage, 0.0), axis=0, keepdims=True)
    TT[0] = tok[...]
    TT[1] = (-token_adv * cot[...].astype(F32)).astype(BF16)

    @pl.when(at_home)
    def _():
        pl.semaphore_wait(barrier, 27)

    @pl.when(jnp.logical_not(at_home))
    def _():
        pl.semaphore_wait(barrier, 28)

    def came(k):
        return rem(z + 8 - NEAR[k], 8)

    def z_copy(a, n, t):
        return remote(
            TT.at[a], XT.at[a, x, own, yh], z_s.at[a, n, t], z_r.at[a, n, yh], at(home, rem(own + NEAR[n], 8), t, x)
        )

    def z_start(a, n):
        for t in range(2):
            @pl.when(jnp.logical_and(jnp.logical_not(is_self(n, t)), jnp.logical_or(n >= 2, t == yh)))
            def _():
                z_copy(a, n, t).start()

    def z_recv(a, k):
        for s in range(2):
            @pl.when(jnp.logical_and(jnp.logical_not(is_self(k, s)), jnp.logical_or(k >= 2, s == yh)))
            def _():
                got = XT.at[a, x, came(k), s]
                remote(got, got, z_s.at[a, k, s], z_r.at[a, k, s], d_right).wait_recv()

    def piece(a, xx, k):
        block = XT.at[a, xx, came(k)]
        return block.at[yh] if k < 2 else block

    def x_copy(a, k, to_right):
        mine = piece(a, x, k)
        if to_right:
            return remote(mine, mine, xr_s.at[a, k], xr_r.at[a, k], d_right)
        return remote(mine, mine, xl_s.at[a, k], xl_r.at[a, k], d_left)

    def x_recv(a, k, from_left):
        got = piece(a, left if from_left else right, k)
        if from_left:
            return remote(got, got, xr_s.at[a, k], xr_r.at[a, k], d_right)
        return remote(got, got, xl_s.at[a, k], xl_r.at[a, k], d_left)

    def f_copy(a, k, to_right):
        got = piece(a, left if to_right else right, k)
        return remote(got, got, f_s.at[a, k], f_r.at[a, k], d_right if to_right else d_left)

    def f_recv(a, k):
        got = piece(a, far, k)
        return remote(got, got, f_s.at[a, k], f_r.at[a, k], d_right)

    def v_copy(a, k, xx):
        mine = XT.at[a, xx, came(k), yh]
        return remote(mine, mine, v_s.at[a, k, xx], v_r.at[a, k, xx], d_y)

    def v_recv(a, k, xx):
        got = XT.at[a, xx, came(k), 1 - yh]
        return remote(got, got, v_s.at[a, k, xx], v_r.at[a, k, xx], d_y)

    def gather_home(a):
        @pl.when(at_home)
        def _():
            XT[a, x, own, yh] = TT[a]

    def forward(a, j):
        x_recv(a, 2 * j, True).wait_recv()
        f_copy(a, 2 * j, True).start()
        x_recv(a, 2 * j + 1, False).wait_recv()
        f_copy(a, 2 * j + 1, False).start()

    def forward_first(a):
        forward(a, 0)
        x_recv(a, 0, False).wait_recv()
        x_recv(a, 1, True).wait_recv()

    def v_start(a, *sides):
        for k in range(2):
            for n in sides:
                v_copy(a, k, n).start()

    def forward_far(a):
        for k in range(2):
            f_recv(a, k).wait_recv()

    def gather_step(a, j):
        for k in (2 * j, 2 * j + 1):
            z_recv(a, k)
            x_copy(a, k, True).start()
            x_copy(a, k, False).start()
            if a == 0:
                z_start(1, k)

    def gather_x(a):
        gather_step(a, 0)
        v_start(0, x)
        gather_step(a, 1)
        gather_step(a, 2)
        forward_first(a)
        v_start(0, left, right)
        gather_step(a, 3)
        forward(a, 1)
        forward(a, 2)

    def gather_end(a):
        for j in range(1, 4):
            x_recv(a, 2 * j, False).wait_recv()
            x_recv(a, 2 * j + 1, True).wait_recv()
            f_recv(a, 2 * j).wait_recv()
            f_recv(a, 2 * j + 1).wait_recv()

        for k in range(2):
            @pl.loop(0, 4)
            def _(n):
                v_recv(a, k, n).wait_recv()

    def gather_drain(a):
        for k in range(8):
            for t in range(2):
                @pl.when(jnp.logical_and(jnp.logical_not(is_self(k, t)), jnp.logical_or(k >= 2, t == yh)))
                def _():
                    z_copy(a, k, t).wait_send()
            x_copy(a, k, True).wait_send()
            x_copy(a, k, False).wait_send()
            f_copy(a, k, k % 2 == 0).wait_send()
        for k in range(2):
            @pl.loop(0, 4)
            def _(n):
                v_copy(a, k, n).wait_send()

    def place(k):
        return rem(z + FAR[k], 8)

    def late(k):
        return k >= 6

    def part(a, xx, k):
        block = PO.at[a, xx, place(k)]
        return block.at[yh] if late(k) else block

    def slot(buf, a, k):
        return buf.at[a, k, 0] if late(k) else buf.at[a, k]

    def u_copy(a, k, n):
        return remote(
            PO.at[a, n, place(k), 1 - yh], RV.at[a, k - 6, n], u_s.at[a, k - 6, n], u_r.at[a, k - 6, n], d_y
        )

    def o_copy(a, k, to_right):
        return remote(
            part(a, far, k), slot(RXO, a, k), o_s.at[a, k], o_r.at[a, k], d_right if to_right else d_left
        )

    def w_copy(a, k, to_right):
        return remote(
            part(a, right if to_right else left, k),
            slot(RXR, a, k), w_s.at[a, k], w_r.at[a, k], d_right if to_right else d_left,
        )

    def c_copy(a, k, to_right):
        return remote(
            part(a, right if to_right else left, k),
            slot(RXC, a, k), c_s.at[a, k], c_r.at[a, k], d_right if to_right else d_left,
        )

    def zz_copy(a, k):
        dst = ZR.at[a, k, yh] if late(k) else ZR.at[a, k]
        return remote(part(a, x, k), dst, zz_s.at[a, k], zz_r.at[a, k], at(dp, place(k), yh, x))

    def q_copy(a, s):
        return remote(YS.at[a, s], FR.at[a, yh], q_s.at[a, s], q_r.at[a, yh], at(home, own, s, x))

    def halves(j):
        return ((2 * j, True), (2 * j + 1, False))

    def o_start(a, j):
        for k, to_right in halves(j):
            o_copy(a, k, to_right).start()

    def w_start(a, j):
        for k, to_right in halves(j):
            w_copy(a, k, not to_right).start()

    def sum_start(a):
        for k in (6, 7):
            @pl.loop(0, 4)
            def _(n):
                u_copy(a, k, n).start()

        o_start(a, 0)
        o_start(a, 1)
        w_start(a, 0)
        if a == 0:
            o_start(a, 2)
            w_start(a, 1)
            w_start(a, 2)

    def fold_y(a):
        for k in (6, 7):
            @pl.loop(0, 4)
            def _(n):
                u_copy(a, k, n).wait_recv()
                mine = PO.at[a, n, place(k), yh]
                mine[...] = (mine[...].astype(F32) + RV[a, k - 6, n].astype(F32)).astype(BF16)

    def combine(a, j):
        for k, to_right in halves(j):
            o_copy(a, k, to_right).wait_recv()
            mine, got = part(a, right if to_right else left, k), slot(RXO, a, k)
            mine[...] = (mine[...].astype(F32) + got[...].astype(F32)).astype(BF16)
            c_copy(a, k, to_right).start()

    def finish(a, j):
        for k, to_right in halves(j):
            w_copy(a, k, not to_right).wait_recv()
            c_copy(a, k, to_right).wait_recv()
            mine = part(a, x, k)
            mine[...] = (
                mine[...].astype(F32) + slot(RXR, a, k)[...].astype(F32) + slot(RXC, a, k)[...].astype(F32)
            ).astype(BF16)
            if k < 7:
                zz_copy(a, k).start()

    def sum_finish(a):
        for j in range(4):
            finish(a, j)

    def sum_z(a):
        for k in range(7):
            zz_copy(a, k).wait_recv()
        for s in range(2):
            total = ZR[a, 0, s].astype(F32)
            for k in range(1, 6):
                total = total + ZR[a, k, s].astype(F32)

            @pl.when(s == yh)
            def _():
                YS[a, s] = (total + ZR[a, 6, s].astype(F32) + PO[a, x, z, s].astype(F32)).astype(BF16)

            @pl.when(s != yh)
            def _():
                YS[a, s] = total.astype(BF16)

            @pl.when(jnp.logical_not(is_self(0, s)))
            def _():
                q_copy(a, s).start()

    def sum_end(a):
        for s in range(2):
            @pl.when(is_self(0, s))
            def _():
                FR[a, s] = YS[a, s]

            @pl.when(jnp.logical_not(is_self(0, s)))
            def _():
                remote(FR.at[a, s], FR.at[a, s], q_s.at[a, s], q_r.at[a, s], d_right).wait_recv()

        (bo, gi)[a][...] = (FR[a, 0].astype(F32) + FR[a, 1].astype(F32)).astype(BF16)

    def sum_drain(a):
        for k in (6, 7):
            @pl.loop(0, 4)
            def _(n):
                u_copy(a, k, n).wait_send()

        for j in range(4):
            for k, to_right in halves(j):
                o_copy(a, k, to_right).wait_send()
                w_copy(a, k, not to_right).wait_send()
                c_copy(a, k, to_right).wait_send()
                if k < 7:
                    zz_copy(a, k).wait_send()

        for s in range(2):
            @pl.when(jnp.logical_not(is_self(0, s)))
            def _():
                q_copy(a, s).wait_send()

    def columns(a, tb):
        return jnp.concatenate(
            [XT[a, xx, 2 * tb + zb, yy] for zb in range(2) for yy in range(2) for xx in range(4)], axis=0
        )

    def scatter_rows(a, tb, total):
        rounded = total.astype(BF16)
        for zb in range(2):
            for yy in range(2):
                for xx in range(4):
                    jb = zb * 8 + yy * 4 + xx
                    PO[a, xx, 2 * tb + zb, yy] = rounded[jb * FB : (jb + 1) * FB]

    def dot(a, b):
        return jnp.dot(a, b, preferred_element_type=F32)

    def weights(w):
        loads[w].wait()
        WB[w] = MW[w].astype(BF16)

        @pl.loop(0, DS // 128)
        def _(n):
            cols = pl.ds(pl.multiple_of(n * 128, 128), 128)
            WT[w, cols, :] = MW[w, :, cols].T.astype(BF16)

    def core_copy(n, src, dst):
        return remote(src, dst, d_s.at[n], d_r.at[n], d_core)

    def chip_copy(n, src, dst):
        return remote(src, dst, e_s.at[n], e_r.at[n], d_chip)

    def grad(left_op, a):
        GR[...] = jnp.zeros((HID, DS), F32)

        @pl.loop(0, 4)
        def _(tb):
            GR[...] += lax.dot_general(
                left_op[tb], columns(a, tb), (((1,), (1,)), ((), ())), preferred_element_type=F32
            )

    def adamw(w, UO, out):
        loads[3 + w].wait()
        loads[6 + w].wait()

        @pl.loop(0, FFS // 8)
        def _(n):
            rows = pl.ds(pl.multiple_of(n * 8, 8), 8)
            gradient = GR[rows, :]
            moment = beta_first * MOM[w, rows, :] + (1.0 - beta_first) * gradient
            second = beta_second * SEC[w, rows, :] + (1.0 - beta_second) * gradient * gradient
            GR[rows, :] = (moment / correct_first) / (
                jnp.sqrt(second / correct_second) + adam_epsilon
            ) + weight_decay * MW[w, rows, :]

        UO[...] = GR[0:FFS, :].astype(BF16)
        store = pltpu.make_async_copy(UO, out, lsem.at[9 + w])
        store.start()
        return store

    gather_home(0)

    for n in range(8):
        z_start(0, n)

    gather_home(1)
    gather_x(0)
    gather_step(1, 0)
    forward_far(0)
    v_start(0, far)
    gather_step(1, 1)
    forward(0, 3)
    for w in range(3):
        weights(w)
    gather_end(0)

    @pl.loop(0, 2)
    def _(k):
        cols = columns(0, 2 * (1 - core) + k)
        SD[k, 0] = dot(WB[0], cols)[:PAD].astype(BF16)
        SD[k, 1] = dot(WB[1], cols)[:PAD].astype(BF16)
        core_copy(8 * k, SD.at[k], RD.at[k]).start()

    @pl.loop(0, 2)
    def _(k):
        cols = columns(0, 2 * core + k)
        core_copy(8 * k, SD.at[k], RD.at[k]).wait_recv()
        gate = dot(WB[0], cols)[:PAD] + RD[k, 0].astype(F32)
        up = dot(WB[1], cols)[:PAD] + RD[k, 1].astype(F32)
        GUO[k, 0] = gate
        GUO[k, 1] = up
        SY[k, 0] = gate.astype(BF16)
        SY[k, 1] = up.astype(BF16)
        chip_copy(k, SY.at[k], RY.at[k]).start()

    gather_step(1, 2)
    forward_first(1)
    gather_step(1, 3)
    forward(1, 1)

    @pl.loop(0, 2)
    def _(k):
        chip_copy(k, SY.at[k], RY.at[k]).wait_recv()
        gate_in = GUO[k, 0] + RY[k, 0].astype(F32)
        up_in = GUO[k, 1] + RY[k, 1].astype(F32)
        sig = jax.nn.sigmoid(gate_in)
        active = gate_in * sig
        ACT[k] = active
        US[k] = up_in * (sig * (1.0 + gate_in * (1.0 - sig)))
        mine = HD.at[2 * core + k]
        HD[2 * core + k, 0:PAD, :] = (active * up_in).astype(BF16)
        core_copy(1 + k, mine, mine).start()

    v_start(1, x, left, right)
    forward(1, 2)

    @pl.loop(0, 2)
    def _(k):
        theirs = HD.at[2 * (1 - core) + k]
        core_copy(1 + k, theirs, theirs).wait_recv()

    @pl.loop(0, 4)
    def _(tb):
        scatter_rows(0, tb, dot(WT[2], HD[tb]))

    forward_far(1)
    v_start(1, far)
    forward(1, 3)
    sum_start(0)
    gather_end(1)

    @pl.loop(0, 2)
    def _(k):
        SD2[k] = dot(WB[2], columns(1, 2 * (1 - core) + k))[:PAD].astype(BF16)

    core_copy(3, SD2, RD2).start()

    @pl.loop(0, 2)
    def _(k):
        DHO[k] = dot(WB[2], columns(1, 2 * core + k))[:PAD]

    core_copy(3, SD2, RD2).wait_recv()

    @pl.loop(0, 2)
    def _(k):
        DHO[k] = DHO[k] + RD2[k].astype(F32)
        SY2[k] = DHO[k].astype(BF16)
        chip_copy(2 + k, SY2.at[k], RY2.at[k]).start()

    combine(0, 0)
    combine(0, 1)
    fold_y(0)
    o_start(0, 3)
    w_start(0, 3)
    combine(0, 2)
    grad(HD, 1)
    store_down = adamw(2, UO2, ud)

    @pl.loop(0, 2)
    def _(k):
        chip_copy(2 + k, SY2.at[k], RY2.at[k]).wait_recv()
        d_hidden = DHO[k] + RY2[k].astype(F32)
        gate, up = DG.at[2 * core + k], DU.at[2 * core + k]
        DG[2 * core + k, 0:PAD, :] = (d_hidden * US[k]).astype(BF16)
        DU[2 * core + k, 0:PAD, :] = (d_hidden * ACT[k]).astype(BF16)
        core_copy(4 + k, gate, gate).start()
        core_copy(6 + k, up, up).start()

    combine(0, 3)

    @pl.loop(0, 2)
    def _(k):
        gate, up = DG.at[2 * (1 - core) + k], DU.at[2 * (1 - core) + k]
        core_copy(4 + k, gate, gate).wait_recv()
        core_copy(6 + k, up, up).wait_recv()

    @pl.loop(0, 4)
    def _(tb):
        scatter_rows(1, tb, dot(WT[0], DG[tb]) + dot(WT[1], DU[tb]))

    sum_start(1)
    sum_finish(0)
    combine(1, 0)
    o_start(1, 2)
    w_start(1, 1)
    grad(DG, 0)
    store_gate = adamw(0, UO0, ug)
    fold_y(1)
    combine(1, 1)
    o_start(1, 3)
    w_start(1, 2)
    finish(1, 0)
    sum_z(0)
    combine(1, 2)
    w_start(1, 3)
    finish(1, 1)
    grad(DU, 0)
    store_up = adamw(1, UO1, uu)
    combine(1, 3)
    finish(1, 2)
    finish(1, 3)
    sum_end(0)
    sum_z(1)
    gather_drain(0)
    gather_drain(1)
    sum_drain(0)
    for k in range(2):
        core_copy(8 * k, SD.at[k], RD.at[k]).wait_send()
    core_copy(3, SD2, RD2).wait_send()

    @pl.loop(0, 2)
    def _(k):
        hid, gate, up = HD.at[2 * core + k], DG.at[2 * core + k], DU.at[2 * core + k]
        chip_copy(k, SY.at[k], RY.at[k]).wait_send()
        chip_copy(2 + k, SY2.at[k], RY2.at[k]).wait_send()
        core_copy(1 + k, hid, hid).wait_send()
        core_copy(4 + k, gate, gate).wait_send()
        core_copy(6 + k, up, up).wait_send()

    sum_end(1)
    sum_drain(1)
    store_down.wait()
    store_gate.wait()
    store_up.wait()


def step(*inputs):
    def vmem(*shape, dtype=BF16):
        return pltpu.VMEM(shape, dtype)

    dma = pltpu.SemaphoreType.DMA
    out = jax.ShapeDtypeStruct
    shard, update = out((FB, TB), BF16), out((FFS, DS), BF16)
    in_vmem = pl.BlockSpec(memory_space=pltpu.VMEM)
    in_any = pl.BlockSpec(memory_space=pl.ANY)
    scratch = [
        vmem(2, FB, TB),
        vmem(2, 4, 8, 2, FB, TB),
        vmem(2, 4, 8, 2, FB, TB),
        vmem(2, 2, 4, FB, TB),
        vmem(2, 8, 2, FB, TB),
        vmem(2, 8, 2, FB, TB),
        vmem(2, 8, 2, FB, TB),
        vmem(2, 8, 2, FB, TB),
        vmem(2, 2, FB, TB),
        vmem(2, 2, FB, TB),
        vmem(3, HID, DS, dtype=F32),
        vmem(3, FFS, DS, dtype=F32),
        vmem(3, FFS, DS, dtype=F32),
        vmem(3, HID, DS),
        vmem(3, DS, HID),
        vmem(4, HID, TB),
        vmem(4, HID, TB),
        vmem(4, HID, TB),
        vmem(2, 2, PAD, TB, dtype=F32),
        vmem(2, PAD, TB, dtype=F32),
        vmem(2, PAD, TB, dtype=F32),
        vmem(2, PAD, TB, dtype=F32),
        vmem(2, 2, PAD, TB),
        vmem(2, 2, PAD, TB),
        vmem(2, 2, PAD, TB),
        vmem(2, 2, PAD, TB),
        vmem(2, PAD, TB),
        vmem(2, PAD, TB),
        vmem(2, PAD, TB),
        vmem(2, PAD, TB),
        vmem(HID, DS, dtype=F32),
        vmem(FFS, DS),
        vmem(FFS, DS),
        vmem(FFS, DS),
        dma((12,)),
        dma((2, 8, 2)), dma((2, 8, 2)),
        dma((2, 8)), dma((2, 8)),
        dma((2, 8)), dma((2, 8)),
        dma((2, 8)), dma((2, 8)),
        dma((2, 2, 4)), dma((2, 2, 4)),
        dma((2, 2, 4)), dma((2, 2, 4)),
        dma((2, 8)), dma((2, 8)),
        dma((2, 8)), dma((2, 8)),
        dma((2, 8)), dma((2, 8)),
        dma((2, 8)), dma((2, 8)),
        dma((2, 2)), dma((2, 2)),
        dma((9,)), dma((9,)),
        dma((4,)), dma((4,)),
    ]
    return pl.pallas_call(
        kernel,
        out_shape=[shard, shard, update, update, update],
        in_specs=[in_vmem] * 5 + [in_any] * 9,
        out_specs=[in_vmem] * 2 + [in_any] * 3,
        scratch_shapes=scratch,
        compiler_params=pltpu.CompilerParams(
            collective_id=0, has_side_effects=True, vmem_limit_bytes=58 * 1024 * 1024
        ),
        cost_estimate=pl.CostEstimate(flops=5_100_000_000, bytes_accessed=12_000_000, transcendentals=1_000_000),
        name="fused_step",
    )(*inputs)


def handing_on(*refs):
    for a, b in zip(refs[:5], refs[5:]):
        b[...] = a[...]


def hand_on(*results):
    in_vmem = pl.BlockSpec(memory_space=pltpu.VMEM)
    return pl.pallas_call(
        handing_on,
        out_shape=[jax.ShapeDtypeStruct(r.shape, r.dtype) for r in results],
        in_specs=[in_vmem] * 5,
        out_specs=[in_vmem] * 5,
        name="hand_on",
    )(*results)


def body(tokens, cotangent, pass_counts, group_ids, token_rollout, *states):
    results = step(
        tokens.T,
        cotangent.T,
        pass_counts.reshape(1, ROLL),
        group_ids.reshape(1, ROLL),
        token_rollout.reshape(1, TB),
        *states,
    )
    block_out, grad_input, update_gate, update_up, update_down = hand_on(*results)
    return block_out.T, grad_input.T, update_gate, update_up, update_down


def solution(mesh):
    act, rep, weight = P("dp", "fsdp"), P(), P("fsdp", "dp")
    return jax.shard_map(
        body,
        mesh=mesh,
        in_specs=(act, act, rep, rep, P("dp")) + (weight,) * 9,
        out_specs=(act, act, weight, weight, weight),
        check_vma=False,
    )
```

```python
import jax
import jax.numpy as jnp
from jax import lax
from jax.experimental import pallas as pl
from jax.experimental.pallas import tpu as pltpu
from jax.sharding import PartitionSpec as P

ROLL = 64
TESTS = 8
beta_first = 0.9
beta_second = 0.95
adam_epsilon = 1e-08
weight_decay = 0.1
correct_first = 1.0 - 0.9**10
correct_second = 1.0 - 0.95**10

FFS = 216
PAD = 224
HID = 256
DS = 1280
FB = 80
TB = 256
NEAR = (0, 1, 7, 2, 6, 3, 5, 4)
FAR = (4, 3, 5, 2, 6, 1, 7, 0)
F32 = jnp.float32
BF16 = jnp.bfloat16


def rem(a, b):
    return lax.rem(a, jnp.int32(b))


def div(a, b):
    return lax.div(a, jnp.int32(b))


def remote(src, dst, send, recv, device):
    return pltpu.make_async_remote_copy(
        src_ref=src,
        dst_ref=dst,
        send_sem=send,
        recv_sem=recv,
        device_id=device,
        device_id_type=pl.DeviceIdType.MESH,
    )


def kernel(
    tok, cot, counts, groups, rolls, mg, mu, md, og, ou, od, sg, su, sd,
    bo, gi, ug, uu, ud,
    TT, COT, CN, GP, RL, XT, PO, RV, RXO, RXR, RXC, ZR, YS, FR,
    MW, MOM, SEC, WB, WT, HD, DG, DU, GUO, ACT, US, DHO,
    SD, RD, SY, RY, SD2, RD2, SY2, RY2, GR, UO0, UO1, UO2,
    lsem, z_s, z_r, xr_s, xr_r, xl_s, xl_r, f_s, f_r,
    v_s, v_r, u_s, u_r, o_s, o_r, w_s, w_r, c_s, c_r, zz_s, zz_r, q_s, q_r,
    d_s, d_r, e_s, e_r,
):
    dp = lax.axis_index("dp")
    fs = lax.axis_index("fsdp")
    z, yh, x = div(fs, 8), rem(div(fs, 4), 2), rem(fs, 4)
    core = rem(dp, 2)
    right, left, far = rem(x + 1, 4), rem(x + 3, 4), rem(x + 2, 4)

    def at(dp_, z_, y_, x_):
        return (dp_, z_ * 8 + y_ * 4 + x_)

    d_right, d_left = at(dp, z, yh, right), at(dp, z, yh, left)
    home = div(z, 2)
    own = 2 * dp + rem(z, 2)
    at_home = home == dp
    d_y = at(dp, z, 1 - yh, x)
    d_core = at(dp + 1 - 2 * core, z, yh, x)
    d_chip = at(rem(dp + 2, 4), z, yh, x)

    def is_self(n, t):
        return jnp.logical_and(jnp.logical_and(at_home, n == 0), t == yh)

    barrier = pltpu.get_barrier_semaphore()

    def greet(peer):
        pl.semaphore_signal(barrier, inc=1, device_id=peer, device_id_type=pl.DeviceIdType.MESH)

    for peer in (d_right, d_left, d_core, d_chip, d_y):
        greet(peer)

    @pl.loop(1, 8)
    def _(n):
        greet(at(dp, rem(z + n, 8), yh, x))

    @pl.loop(0, 8)
    def _(n):
        for t in range(2):
            @pl.when(jnp.logical_not(is_self(n, t)))
            def _():
                greet(at(div(rem(z + n, 8), 2), 2 * dp + rem(z + n, 2), t, x))

    smalls = []
    for n, (src, dst) in enumerate(zip((tok, cot, counts, groups, rolls), (TT.at[0], COT, CN, GP, RL))):
        smalls.append(pltpu.make_async_copy(src, dst, lsem.at[12 + n]))
    for small in smalls:
        small.start()
    srcs = (mg, mu, md, og, ou, od, sg, su, sd)
    loads = []
    for n, src in enumerate(srcs):
        dst = (MW, MOM, SEC)[n // 3].at[n % 3, pl.ds(0, FFS)]
        loads.append(pltpu.make_async_copy(src, dst, lsem.at[n]))
    for load in loads:
        load.start()

    for w in range(3):
        MW[w, FFS:HID, :] = jnp.zeros((HID - FFS, DS), F32)
    for buf in (HD, DG, DU):
        for n in range(2):
            buf[2 * core + n, PAD:HID, :] = jnp.zeros((HID - PAD, TB), BF16)

    for small in smalls:
        small.wait()

    reward = CN[...].astype(F32) / TESTS
    group = GP[...].astype(F32)
    group_col = jnp.broadcast_to(group, (ROLL, ROLL)).T
    same = (group_col == group).astype(F32)
    baseline = jnp.sum(same * reward, axis=1, keepdims=True) / jnp.sum(same, axis=1, keepdims=True)
    reward_col = jnp.broadcast_to(reward, (ROLL, ROLL)).T[:, 0:1]
    advantage = reward_col - baseline
    rollout = lax.broadcasted_iota(jnp.int32, (ROLL, TB), 0)
    token_adv = jnp.sum(jnp.where(rollout == RL[...], advantage, 0.0), axis=0, keepdims=True)
    TT[1] = (-token_adv * COT[...].astype(F32)).astype(BF16)

    @pl.when(at_home)
    def _():
        pl.semaphore_wait(barrier, 27)

    @pl.when(jnp.logical_not(at_home))
    def _():
        pl.semaphore_wait(barrier, 28)

    def came(k):
        return rem(z + 8 - NEAR[k], 8)

    def z_copy(a, n, t):
        return remote(
            TT.at[a], XT.at[a, x, own, yh], z_s.at[a, n, t], z_r.at[a, n, yh], at(home, rem(own + NEAR[n], 8), t, x)
        )

    def z_start(a, n):
        for t in range(2):
            @pl.when(jnp.logical_and(jnp.logical_not(is_self(n, t)), jnp.logical_or(n >= 2, t == yh)))
            def _():
                z_copy(a, n, t).start()

    def z_recv(a, k):
        for s in range(2):
            @pl.when(jnp.logical_and(jnp.logical_not(is_self(k, s)), jnp.logical_or(k >= 2, s == yh)))
            def _():
                got = XT.at[a, x, came(k), s]
                remote(got, got, z_s.at[a, k, s], z_r.at[a, k, s], d_right).wait_recv()

    def piece(a, xx, k):
        block = XT.at[a, xx, came(k)]
        return block.at[yh] if k < 2 else block

    def x_copy(a, k, to_right):
        mine = piece(a, x, k)
        if to_right:
            return remote(mine, mine, xr_s.at[a, k], xr_r.at[a, k], d_right)
        return remote(mine, mine, xl_s.at[a, k], xl_r.at[a, k], d_left)

    def x_recv(a, k, from_left):
        got = piece(a, left if from_left else right, k)
        if from_left:
            return remote(got, got, xr_s.at[a, k], xr_r.at[a, k], d_right)
        return remote(got, got, xl_s.at[a, k], xl_r.at[a, k], d_left)

    def f_copy(a, k, to_right):
        got = piece(a, left if to_right else right, k)
        return remote(got, got, f_s.at[a, k], f_r.at[a, k], d_right if to_right else d_left)

    def f_recv(a, k):
        got = piece(a, far, k)
        return remote(got, got, f_s.at[a, k], f_r.at[a, k], d_right)

    def v_copy(a, k, xx):
        mine = XT.at[a, xx, came(k), yh]
        return remote(mine, mine, v_s.at[a, k, xx], v_r.at[a, k, xx], d_y)

    def v_recv(a, k, xx):
        got = XT.at[a, xx, came(k), 1 - yh]
        return remote(got, got, v_s.at[a, k, xx], v_r.at[a, k, xx], d_y)

    def gather_home(a):
        @pl.when(at_home)
        def _():
            XT[a, x, own, yh] = TT[a]

    def forward(a, j):
        x_recv(a, 2 * j, True).wait_recv()
        f_copy(a, 2 * j, True).start()
        x_recv(a, 2 * j + 1, False).wait_recv()
        f_copy(a, 2 * j + 1, False).start()

    def forward_first(a):
        forward(a, 0)
        x_recv(a, 0, False).wait_recv()
        x_recv(a, 1, True).wait_recv()

    def v_start(a, *sides):
        for k in range(2):
            for n in sides:
                v_copy(a, k, n).start()

    def forward_far(a):
        for k in range(2):
            f_recv(a, k).wait_recv()

    def gather_step(a, j):
        for k in (2 * j, 2 * j + 1):
            z_recv(a, k)
            x_copy(a, k, True).start()
            x_copy(a, k, False).start()
            if a == 0:
                z_start(1, k)

    def gather_x(a):
        gather_step(a, 0)
        v_start(0, x)
        gather_step(a, 1)
        gather_step(a, 2)
        forward_first(a)
        v_start(0, left, right)
        gather_step(a, 3)
        forward(a, 1)
        forward(a, 2)

    def gather_end(a):
        for j in range(1, 4):
            x_recv(a, 2 * j, False).wait_recv()
            x_recv(a, 2 * j + 1, True).wait_recv()
            f_recv(a, 2 * j).wait_recv()
            f_recv(a, 2 * j + 1).wait_recv()

        for k in range(2):
            @pl.loop(0, 4)
            def _(n):
                v_recv(a, k, n).wait_recv()

    def gather_drain(a):
        for k in range(8):
            for t in range(2):
                @pl.when(jnp.logical_and(jnp.logical_not(is_self(k, t)), jnp.logical_or(k >= 2, t == yh)))
                def _():
                    z_copy(a, k, t).wait_send()
            x_copy(a, k, True).wait_send()
            x_copy(a, k, False).wait_send()
            f_copy(a, k, k % 2 == 0).wait_send()
        for k in range(2):
            @pl.loop(0, 4)
            def _(n):
                v_copy(a, k, n).wait_send()

    def place(k):
        return rem(z + FAR[k], 8)

    def late(k):
        return k >= 6

    def part(a, xx, k):
        block = PO.at[a, xx, place(k)]
        return block.at[yh] if late(k) else block

    def slot(buf, a, k):
        return buf.at[a, k, 0] if late(k) else buf.at[a, k]

    def u_copy(a, k, n):
        return remote(
            PO.at[a, n, place(k), 1 - yh], RV.at[a, k - 6, n], u_s.at[a, k - 6, n], u_r.at[a, k - 6, n], d_y
        )

    def o_copy(a, k, to_right):
        return remote(
            part(a, far, k), slot(RXO, a, k), o_s.at[a, k], o_r.at[a, k], d_right if to_right else d_left
        )

    def w_copy(a, k, to_right):
        return remote(
            part(a, right if to_right else left, k),
            slot(RXR, a, k), w_s.at[a, k], w_r.at[a, k], d_right if to_right else d_left,
        )

    def c_copy(a, k, to_right):
        return remote(
            part(a, right if to_right else left, k),
            slot(RXC, a, k), c_s.at[a, k], c_r.at[a, k], d_right if to_right else d_left,
        )

    def zz_copy(a, k):
        dst = ZR.at[a, k, yh] if late(k) else ZR.at[a, k]
        return remote(part(a, x, k), dst, zz_s.at[a, k], zz_r.at[a, k], at(dp, place(k), yh, x))

    def q_copy(a, s):
        return remote(YS.at[a, s], FR.at[a, yh], q_s.at[a, s], q_r.at[a, yh], at(home, own, s, x))

    def halves(j):
        return ((2 * j, True), (2 * j + 1, False))

    def o_start(a, j):
        for k, to_right in halves(j):
            o_copy(a, k, to_right).start()

    def w_start(a, j):
        for k, to_right in halves(j):
            w_copy(a, k, not to_right).start()

    def sum_start(a):
        for k in (6, 7):
            @pl.loop(0, 4)
            def _(n):
                u_copy(a, k, n).start()

        o_start(a, 0)
        o_start(a, 1)
        w_start(a, 0)
        if a == 0:
            o_start(a, 2)
            w_start(a, 1)
            w_start(a, 2)

    def fold_y(a):
        for k in (6, 7):
            @pl.loop(0, 4)
            def _(n):
                u_copy(a, k, n).wait_recv()
                mine = PO.at[a, n, place(k), yh]
                mine[...] = (mine[...].astype(F32) + RV[a, k - 6, n].astype(F32)).astype(BF16)

    def combine(a, j):
        for k, to_right in halves(j):
            o_copy(a, k, to_right).wait_recv()
            mine, got = part(a, right if to_right else left, k), slot(RXO, a, k)
            mine[...] = (mine[...].astype(F32) + got[...].astype(F32)).astype(BF16)
            c_copy(a, k, to_right).start()

    def finish(a, j):
        for k, to_right in halves(j):
            w_copy(a, k, not to_right).wait_recv()
            c_copy(a, k, to_right).wait_recv()
            mine = part(a, x, k)
            mine[...] = (
                mine[...].astype(F32) + slot(RXR, a, k)[...].astype(F32) + slot(RXC, a, k)[...].astype(F32)
            ).astype(BF16)
            if k < 7:
                zz_copy(a, k).start()

    def sum_finish(a):
        for j in range(4):
            finish(a, j)

    def sum_z(a):
        for k in range(7):
            zz_copy(a, k).wait_recv()
        for s in range(2):
            total = ZR[a, 0, s].astype(F32)
            for k in range(1, 6):
                total = total + ZR[a, k, s].astype(F32)

            @pl.when(s == yh)
            def _():
                YS[a, s] = (total + ZR[a, 6, s].astype(F32) + PO[a, x, z, s].astype(F32)).astype(BF16)

            @pl.when(s != yh)
            def _():
                YS[a, s] = total.astype(BF16)

            @pl.when(jnp.logical_not(is_self(0, s)))
            def _():
                q_copy(a, s).start()

    def sum_end(a):
        for s in range(2):
            @pl.when(is_self(0, s))
            def _():
                FR[a, s] = YS[a, s]

            @pl.when(jnp.logical_not(is_self(0, s)))
            def _():
                remote(FR.at[a, s], FR.at[a, s], q_s.at[a, s], q_r.at[a, s], d_right).wait_recv()

        (bo, gi)[a][...] = (FR[a, 0].astype(F32) + FR[a, 1].astype(F32)).astype(BF16)

    def sum_drain(a):
        for k in (6, 7):
            @pl.loop(0, 4)
            def _(n):
                u_copy(a, k, n).wait_send()

        for j in range(4):
            for k, to_right in halves(j):
                o_copy(a, k, to_right).wait_send()
                w_copy(a, k, not to_right).wait_send()
                c_copy(a, k, to_right).wait_send()
                if k < 7:
                    zz_copy(a, k).wait_send()

        for s in range(2):
            @pl.when(jnp.logical_not(is_self(0, s)))
            def _():
                q_copy(a, s).wait_send()

    def columns(a, tb):
        return jnp.concatenate(
            [XT[a, xx, 2 * tb + zb, yy] for zb in range(2) for yy in range(2) for xx in range(4)], axis=0
        )

    def scatter_rows(a, tb, total):
        rounded = total.astype(BF16)
        for zb in range(2):
            for yy in range(2):
                for xx in range(4):
                    jb = zb * 8 + yy * 4 + xx
                    PO[a, xx, 2 * tb + zb, yy] = rounded[jb * FB : (jb + 1) * FB]

    def dot(a, b):
        return jnp.dot(a, b, preferred_element_type=F32)

    def weights(w):
        loads[w].wait()
        WB[w] = MW[w].astype(BF16)

        @pl.loop(0, DS // 128)
        def _(n):
            cols = pl.ds(pl.multiple_of(n * 128, 128), 128)
            WT[w, cols, :] = MW[w, :, cols].T.astype(BF16)

    def core_copy(n, src, dst):
        return remote(src, dst, d_s.at[n], d_r.at[n], d_core)

    def chip_copy(n, src, dst):
        return remote(src, dst, e_s.at[n], e_r.at[n], d_chip)

    def grad(left_op, a):
        GR[...] = jnp.zeros((HID, DS), F32)

        @pl.loop(0, 4)
        def _(tb):
            GR[...] += lax.dot_general(
                left_op[tb], columns(a, tb), (((1,), (1,)), ((), ())), preferred_element_type=F32
            )

    def adamw(w, UO, out):
        loads[3 + w].wait()
        loads[6 + w].wait()

        @pl.loop(0, FFS // 8)
        def _(n):
            rows = pl.ds(pl.multiple_of(n * 8, 8), 8)
            gradient = GR[rows, :]
            moment = beta_first * MOM[w, rows, :] + (1.0 - beta_first) * gradient
            second = beta_second * SEC[w, rows, :] + (1.0 - beta_second) * gradient * gradient
            GR[rows, :] = (moment / correct_first) / (
                jnp.sqrt(second / correct_second) + adam_epsilon
            ) + weight_decay * MW[w, rows, :]

        UO[...] = GR[0:FFS, :].astype(BF16)
        store = pltpu.make_async_copy(UO, out, lsem.at[9 + w])
        store.start()
        return store

    gather_home(0)

    for n in range(8):
        z_start(0, n)

    gather_home(1)
    gather_x(0)
    gather_step(1, 0)
    forward_far(0)
    v_start(0, far)
    gather_step(1, 1)
    forward(0, 3)
    for w in range(3):
        weights(w)
    gather_end(0)

    @pl.loop(0, 2)
    def _(k):
        cols = columns(0, 2 * (1 - core) + k)
        SD[k, 0] = dot(WB[0], cols)[:PAD].astype(BF16)
        SD[k, 1] = dot(WB[1], cols)[:PAD].astype(BF16)
        core_copy(8 * k, SD.at[k], RD.at[k]).start()

    @pl.loop(0, 2)
    def _(k):
        cols = columns(0, 2 * core + k)
        core_copy(8 * k, SD.at[k], RD.at[k]).wait_recv()
        gate = dot(WB[0], cols)[:PAD] + RD[k, 0].astype(F32)
        up = dot(WB[1], cols)[:PAD] + RD[k, 1].astype(F32)
        GUO[k, 0] = gate
        GUO[k, 1] = up
        SY[k, 0] = gate.astype(BF16)
        SY[k, 1] = up.astype(BF16)
        chip_copy(k, SY.at[k], RY.at[k]).start()

    gather_step(1, 2)
    forward_first(1)
    gather_step(1, 3)
    forward(1, 1)

    @pl.loop(0, 2)
    def _(k):
        chip_copy(k, SY.at[k], RY.at[k]).wait_recv()
        gate_in = GUO[k, 0] + RY[k, 0].astype(F32)
        up_in = GUO[k, 1] + RY[k, 1].astype(F32)
        sig = jax.nn.sigmoid(gate_in)
        active = gate_in * sig
        ACT[k] = active
        US[k] = up_in * (sig * (1.0 + gate_in * (1.0 - sig)))
        mine = HD.at[2 * core + k]
        HD[2 * core + k, 0:PAD, :] = (active * up_in).astype(BF16)
        core_copy(1 + k, mine, mine).start()

    v_start(1, x, left, right)
    forward(1, 2)

    @pl.loop(0, 2)
    def _(k):
        theirs = HD.at[2 * (1 - core) + k]
        core_copy(1 + k, theirs, theirs).wait_recv()

    @pl.loop(0, 4)
    def _(tb):
        scatter_rows(0, tb, dot(WT[2], HD[tb]))

    forward_far(1)
    v_start(1, far)
    forward(1, 3)
    sum_start(0)
    gather_end(1)

    @pl.loop(0, 2)
    def _(k):
        SD2[k] = dot(WB[2], columns(1, 2 * (1 - core) + k))[:PAD].astype(BF16)

    core_copy(3, SD2, RD2).start()

    @pl.loop(0, 2)
    def _(k):
        DHO[k] = dot(WB[2], columns(1, 2 * core + k))[:PAD]

    core_copy(3, SD2, RD2).wait_recv()

    @pl.loop(0, 2)
    def _(k):
        DHO[k] = DHO[k] + RD2[k].astype(F32)
        SY2[k] = DHO[k].astype(BF16)
        chip_copy(2 + k, SY2.at[k], RY2.at[k]).start()

    combine(0, 0)
    combine(0, 1)
    fold_y(0)
    o_start(0, 3)
    w_start(0, 3)
    combine(0, 2)
    grad(HD, 1)
    store_down = adamw(2, UO2, ud)

    @pl.loop(0, 2)
    def _(k):
        chip_copy(2 + k, SY2.at[k], RY2.at[k]).wait_recv()
        d_hidden = DHO[k] + RY2[k].astype(F32)
        gate, up = DG.at[2 * core + k], DU.at[2 * core + k]
        DG[2 * core + k, 0:PAD, :] = (d_hidden * US[k]).astype(BF16)
        DU[2 * core + k, 0:PAD, :] = (d_hidden * ACT[k]).astype(BF16)
        core_copy(4 + k, gate, gate).start()
        core_copy(6 + k, up, up).start()

    combine(0, 3)

    @pl.loop(0, 2)
    def _(k):
        gate, up = DG.at[2 * (1 - core) + k], DU.at[2 * (1 - core) + k]
        core_copy(4 + k, gate, gate).wait_recv()
        core_copy(6 + k, up, up).wait_recv()

    @pl.loop(0, 4)
    def _(tb):
        scatter_rows(1, tb, dot(WT[0], DG[tb]) + dot(WT[1], DU[tb]))

    sum_start(1)
    sum_finish(0)
    combine(1, 0)
    o_start(1, 2)
    w_start(1, 1)
    grad(DG, 0)
    store_gate = adamw(0, UO0, ug)
    fold_y(1)
    combine(1, 1)
    o_start(1, 3)
    w_start(1, 2)
    finish(1, 0)
    sum_z(0)
    combine(1, 2)
    w_start(1, 3)
    finish(1, 1)
    grad(DU, 0)
    store_up = adamw(1, UO1, uu)
    combine(1, 3)
    finish(1, 2)
    finish(1, 3)
    sum_end(0)
    sum_z(1)
    gather_drain(0)
    gather_drain(1)
    sum_drain(0)
    for k in range(2):
        core_copy(8 * k, SD.at[k], RD.at[k]).wait_send()
    core_copy(3, SD2, RD2).wait_send()

    @pl.loop(0, 2)
    def _(k):
        hid, gate, up = HD.at[2 * core + k], DG.at[2 * core + k], DU.at[2 * core + k]
        chip_copy(k, SY.at[k], RY.at[k]).wait_send()
        chip_copy(2 + k, SY2.at[k], RY2.at[k]).wait_send()
        core_copy(1 + k, hid, hid).wait_send()
        core_copy(4 + k, gate, gate).wait_send()
        core_copy(6 + k, up, up).wait_send()

    sum_end(1)
    sum_drain(1)
    store_down.wait()
    store_gate.wait()
    store_up.wait()


def step(*inputs):
    def vmem(*shape, dtype=BF16):
        return pltpu.VMEM(shape, dtype)

    dma = pltpu.SemaphoreType.DMA
    out = jax.ShapeDtypeStruct
    shard, update = out((FB, TB), BF16), out((FFS, DS), BF16)
    in_vmem = pl.BlockSpec(memory_space=pltpu.VMEM)
    in_any = pl.BlockSpec(memory_space=pl.ANY)
    scratch = [
        vmem(2, FB, TB),
        vmem(FB, TB),
        vmem(1, ROLL, dtype=jnp.int32),
        vmem(1, ROLL, dtype=jnp.int32),
        vmem(1, TB, dtype=jnp.int32),
        vmem(2, 4, 8, 2, FB, TB),
        vmem(2, 4, 8, 2, FB, TB),
        vmem(2, 2, 4, FB, TB),
        vmem(2, 8, 2, FB, TB),
        vmem(2, 8, 2, FB, TB),
        vmem(2, 8, 2, FB, TB),
        vmem(2, 8, 2, FB, TB),
        vmem(2, 2, FB, TB),
        vmem(2, 2, FB, TB),
        vmem(3, HID, DS, dtype=F32),
        vmem(3, FFS, DS, dtype=F32),
        vmem(3, FFS, DS, dtype=F32),
        vmem(3, HID, DS),
        vmem(3, DS, HID),
        vmem(4, HID, TB),
        vmem(4, HID, TB),
        vmem(4, HID, TB),
        vmem(2, 2, PAD, TB, dtype=F32),
        vmem(2, PAD, TB, dtype=F32),
        vmem(2, PAD, TB, dtype=F32),
        vmem(2, PAD, TB, dtype=F32),
        vmem(2, 2, PAD, TB),
        vmem(2, 2, PAD, TB),
        vmem(2, 2, PAD, TB),
        vmem(2, 2, PAD, TB),
        vmem(2, PAD, TB),
        vmem(2, PAD, TB),
        vmem(2, PAD, TB),
        vmem(2, PAD, TB),
        vmem(HID, DS, dtype=F32),
        vmem(FFS, DS),
        vmem(FFS, DS),
        vmem(FFS, DS),
        dma((17,)),
        dma((2, 8, 2)), dma((2, 8, 2)),
        dma((2, 8)), dma((2, 8)),
        dma((2, 8)), dma((2, 8)),
        dma((2, 8)), dma((2, 8)),
        dma((2, 2, 4)), dma((2, 2, 4)),
        dma((2, 2, 4)), dma((2, 2, 4)),
        dma((2, 8)), dma((2, 8)),
        dma((2, 8)), dma((2, 8)),
        dma((2, 8)), dma((2, 8)),
        dma((2, 8)), dma((2, 8)),
        dma((2, 2)), dma((2, 2)),
        dma((9,)), dma((9,)),
        dma((4,)), dma((4,)),
    ]
    return pl.pallas_call(
        kernel,
        out_shape=[shard, shard, update, update, update],
        in_specs=[in_any] * 14,
        out_specs=[in_vmem] * 2 + [in_any] * 3,
        scratch_shapes=scratch,
        compiler_params=pltpu.CompilerParams(
            collective_id=0, has_side_effects=True, vmem_limit_bytes=58 * 1024 * 1024
        ),
        cost_estimate=pl.CostEstimate(flops=5_100_000_000, bytes_accessed=12_000_000, transcendentals=1_000_000),
        name="fused_step",
    )(*inputs)


def handing_on(*refs):
    for a, b in zip(refs[:5], refs[5:]):
        b[...] = a[...]


def hand_on(*results):
    in_vmem = pl.BlockSpec(memory_space=pltpu.VMEM)
    return pl.pallas_call(
        handing_on,
        out_shape=[jax.ShapeDtypeStruct(r.shape, r.dtype) for r in results],
        in_specs=[in_vmem] * 5,
        out_specs=[in_vmem] * 5,
        name="hand_on",
    )(*results)


def body(tokens, cotangent, pass_counts, group_ids, token_rollout, *states):
    results = step(
        tokens.T,
        cotangent.T,
        pass_counts.reshape(1, ROLL),
        group_ids.reshape(1, ROLL),
        token_rollout.reshape(1, TB),
        *states,
    )
    block_out, grad_input, update_gate, update_up, update_down = hand_on(*results)
    return block_out.T, grad_input.T, update_gate, update_up, update_down


def solution(mesh):
    act, rep, weight = P("dp", "fsdp"), P(), P("fsdp", "dp")
    return jax.shard_map(
        body,
        mesh=mesh,
        in_specs=(act, act, rep, rep, P("dp")) + (weight,) * 9,
        out_specs=(act, act, weight, weight, weight),
        check_vma=False,
    )
```

```python
import jax
import jax.numpy as jnp
from jax import lax
from jax.experimental import pallas as pl
from jax.experimental.pallas import tpu as pltpu
from jax.sharding import PartitionSpec as P

ROLL = 64
TESTS = 8
beta_first = 0.9
beta_second = 0.95
adam_epsilon = 1e-08
weight_decay = 0.1
correct_first = 1.0 - 0.9**10
correct_second = 1.0 - 0.95**10

FFS = 216
PAD = 224
HID = 256
DS = 1280
FB = 80
TB = 256
NEAR = (0, 1, 7, 2, 6, 3, 5, 4)
FAR = (4, 3, 5, 2, 6, 1, 7, 0)
F32 = jnp.float32
BF16 = jnp.bfloat16


def rem(a, b):
    return lax.rem(a, jnp.int32(b))


def div(a, b):
    return lax.div(a, jnp.int32(b))


def remote(src, dst, send, recv, device):
    return pltpu.make_async_remote_copy(
        src_ref=src,
        dst_ref=dst,
        send_sem=send,
        recv_sem=recv,
        device_id=device,
        device_id_type=pl.DeviceIdType.MESH,
    )


def kernel(
    tok, cot, counts, groups, rolls, mg, mu, md, og, ou, od, sg, su, sd,
    bo, gi, ug, uu, ud,
    TT, COT, CN, GP, RL, XT, PO, RV, RXO, RXR, RXC, ZR, YS, FR,
    MW, MOM, SEC, WB, WT, HD, DG, DU, GUO, ACT, US, DHO,
    SD, RD, SY, RY, SD2, RD2, SY2, RY2, GR, UO0, UO1, UO2,
    lsem, z_s, z_r, xr_s, xr_r, xl_s, xl_r, f_s, f_r,
    v_s, v_r, u_s, u_r, o_s, o_r, w_s, w_r, c_s, c_r, zz_s, zz_r, q_s, q_r,
    d_s, d_r, e_s, e_r,
):
    dp = lax.axis_index("dp")
    fs = lax.axis_index("fsdp")
    z, yh, x = div(fs, 8), rem(div(fs, 4), 2), rem(fs, 4)
    core = rem(dp, 2)
    right, left, far = rem(x + 1, 4), rem(x + 3, 4), rem(x + 2, 4)

    def at(dp_, z_, y_, x_):
        return (dp_, z_ * 8 + y_ * 4 + x_)

    d_right, d_left = at(dp, z, yh, right), at(dp, z, yh, left)
    home = div(z, 2)
    own = 2 * dp + rem(z, 2)
    at_home = home == dp
    d_y = at(dp, z, 1 - yh, x)
    d_core = at(dp + 1 - 2 * core, z, yh, x)
    d_chip = at(rem(dp + 2, 4), z, yh, x)

    def is_self(n, t):
        return jnp.logical_and(jnp.logical_and(at_home, n == 0), t == yh)

    barrier = pltpu.get_barrier_semaphore()

    def greet(peer):
        pl.semaphore_signal(barrier, inc=1, device_id=peer, device_id_type=pl.DeviceIdType.MESH)

    for peer in (d_right, d_left, d_core, d_chip, d_y):
        greet(peer)

    @pl.loop(1, 8)
    def _(n):
        greet(at(dp, rem(z + n, 8), yh, x))

    @pl.loop(0, 8)
    def _(n):
        for t in range(2):
            @pl.when(jnp.logical_not(is_self(n, t)))
            def _():
                greet(at(div(rem(z + n, 8), 2), 2 * dp + rem(z + n, 2), t, x))

    smalls = []
    for n, (src, dst) in enumerate(zip((tok, cot, counts, groups, rolls), (TT.at[0], COT, CN, GP, RL))):
        smalls.append(pltpu.make_async_copy(src, dst, lsem.at[12 + n]))
    for small in smalls:
        small.start()
    srcs = (mg, mu, md, og, ou, od, sg, su, sd)
    loads = []
    for n, src in enumerate(srcs):
        dst = (MW, MOM, SEC)[n // 3].at[n % 3, pl.ds(0, FFS)]
        loads.append(pltpu.make_async_copy(src, dst, lsem.at[n]))
    for load in loads:
        load.start()

    for w in range(3):
        MW[w, FFS:HID, :] = jnp.zeros((HID - FFS, DS), F32)
    for buf in (HD, DG, DU):
        for n in range(2):
            buf[2 * core + n, PAD:HID, :] = jnp.zeros((HID - PAD, TB), BF16)

    for small in smalls:
        small.wait()

    reward = CN[...].astype(F32) / TESTS
    group = GP[...].astype(F32)
    group_col = jnp.broadcast_to(group, (ROLL, ROLL)).T
    same = (group_col == group).astype(F32)
    baseline = jnp.sum(same * reward, axis=1, keepdims=True) / jnp.sum(same, axis=1, keepdims=True)
    reward_col = jnp.broadcast_to(reward, (ROLL, ROLL)).T[:, 0:1]
    advantage = reward_col - baseline
    rollout = lax.broadcasted_iota(jnp.int32, (ROLL, TB), 0)
    token_adv = jnp.sum(jnp.where(rollout == RL[...], advantage, 0.0), axis=0, keepdims=True)
    TT[1] = (-token_adv * COT[...].astype(F32)).astype(BF16)

    @pl.when(at_home)
    def _():
        pl.semaphore_wait(barrier, 27)

    @pl.when(jnp.logical_not(at_home))
    def _():
        pl.semaphore_wait(barrier, 28)

    def came(k):
        return rem(z + 8 - NEAR[k], 8)

    def z_copy(a, n, t):
        return remote(
            TT.at[a], XT.at[a, x, own, yh], z_s.at[a, n, t], z_r.at[a, n, yh], at(home, rem(own + NEAR[n], 8), t, x)
        )

    def z_start(a, n):
        for t in range(2):
            @pl.when(jnp.logical_and(jnp.logical_not(is_self(n, t)), jnp.logical_or(n >= 2, t == yh)))
            def _():
                z_copy(a, n, t).start()

    def z_recv(a, k):
        for s in range(2):
            @pl.when(jnp.logical_and(jnp.logical_not(is_self(k, s)), jnp.logical_or(k >= 2, s == yh)))
            def _():
                got = XT.at[a, x, came(k), s]
                remote(got, got, z_s.at[a, k, s], z_r.at[a, k, s], d_right).wait_recv()

    def piece(a, xx, k):
        block = XT.at[a, xx, came(k)]
        return block.at[yh] if k < 2 else block

    def x_copy(a, k, to_right):
        mine = piece(a, x, k)
        if to_right:
            return remote(mine, mine, xr_s.at[a, k], xr_r.at[a, k], d_right)
        return remote(mine, mine, xl_s.at[a, k], xl_r.at[a, k], d_left)

    def x_recv(a, k, from_left):
        got = piece(a, left if from_left else right, k)
        if from_left:
            return remote(got, got, xr_s.at[a, k], xr_r.at[a, k], d_right)
        return remote(got, got, xl_s.at[a, k], xl_r.at[a, k], d_left)

    def f_copy(a, k, to_right):
        got = piece(a, left if to_right else right, k)
        return remote(got, got, f_s.at[a, k], f_r.at[a, k], d_right if to_right else d_left)

    def f_recv(a, k):
        got = piece(a, far, k)
        return remote(got, got, f_s.at[a, k], f_r.at[a, k], d_right)

    def v_copy(a, k, xx):
        mine = XT.at[a, xx, came(k), yh]
        return remote(mine, mine, v_s.at[a, k, xx], v_r.at[a, k, xx], d_y)

    def v_recv(a, k, xx):
        got = XT.at[a, xx, came(k), 1 - yh]
        return remote(got, got, v_s.at[a, k, xx], v_r.at[a, k, xx], d_y)

    def gather_home(a):
        @pl.when(at_home)
        def _():
            XT[a, x, own, yh] = TT[a]

    def forward(a, j):
        x_recv(a, 2 * j, True).wait_recv()
        f_copy(a, 2 * j, True).start()
        x_recv(a, 2 * j + 1, False).wait_recv()
        f_copy(a, 2 * j + 1, False).start()

    def forward_first(a):
        forward(a, 0)
        x_recv(a, 0, False).wait_recv()
        x_recv(a, 1, True).wait_recv()

    def v_start(a, *sides):
        for k in range(2):
            for n in sides:
                v_copy(a, k, n).start()

    def forward_far(a):
        for k in range(2):
            f_recv(a, k).wait_recv()

    def gather_step(a, j):
        for k in (2 * j, 2 * j + 1):
            z_recv(a, k)
            x_copy(a, k, True).start()
            x_copy(a, k, False).start()
            if a == 0:
                z_start(1, k)

    def gather_x(a):
        gather_step(a, 0)
        v_start(0, x)
        gather_step(a, 1)
        gather_step(a, 2)
        forward_first(a)
        v_start(0, left, right)
        gather_step(a, 3)
        forward(a, 1)
        forward(a, 2)

    def gather_end(a):
        for j in range(1, 4):
            x_recv(a, 2 * j, False).wait_recv()
            x_recv(a, 2 * j + 1, True).wait_recv()
            f_recv(a, 2 * j).wait_recv()
            f_recv(a, 2 * j + 1).wait_recv()

        for k in range(2):
            @pl.loop(0, 4)
            def _(n):
                v_recv(a, k, n).wait_recv()

    def gather_drain(a):
        for k in range(8):
            for t in range(2):
                @pl.when(jnp.logical_and(jnp.logical_not(is_self(k, t)), jnp.logical_or(k >= 2, t == yh)))
                def _():
                    z_copy(a, k, t).wait_send()
            x_copy(a, k, True).wait_send()
            x_copy(a, k, False).wait_send()
            f_copy(a, k, k % 2 == 0).wait_send()
        for k in range(2):
            @pl.loop(0, 4)
            def _(n):
                v_copy(a, k, n).wait_send()

    def place(k):
        return rem(z + FAR[k], 8)

    def late(k):
        return k >= 6

    def part(a, xx, k):
        block = PO.at[a, xx, place(k)]
        return block.at[yh] if late(k) else block

    def slot(buf, a, k):
        return buf.at[a, k, 0] if late(k) else buf.at[a, k]

    def u_copy(a, k, n):
        return remote(
            PO.at[a, n, place(k), 1 - yh], RV.at[a, k - 6, n], u_s.at[a, k - 6, n], u_r.at[a, k - 6, n], d_y
        )

    def o_copy(a, k, to_right):
        return remote(
            part(a, far, k), slot(RXO, a, k), o_s.at[a, k], o_r.at[a, k], d_right if to_right else d_left
        )

    def w_copy(a, k, to_right):
        return remote(
            part(a, right if to_right else left, k),
            slot(RXR, a, k), w_s.at[a, k], w_r.at[a, k], d_right if to_right else d_left,
        )

    def c_copy(a, k, to_right):
        return remote(
            part(a, right if to_right else left, k),
            slot(RXC, a, k), c_s.at[a, k], c_r.at[a, k], d_right if to_right else d_left,
        )

    def zz_copy(a, k):
        dst = ZR.at[a, k, yh] if late(k) else ZR.at[a, k]
        return remote(part(a, x, k), dst, zz_s.at[a, k], zz_r.at[a, k], at(dp, place(k), yh, x))

    def q_copy(a, s):
        return remote(YS.at[a, s], FR.at[a, yh], q_s.at[a, s], q_r.at[a, yh], at(home, own, s, x))

    def halves(j):
        return ((2 * j, True), (2 * j + 1, False))

    def o_start(a, j):
        for k, to_right in halves(j):
            o_copy(a, k, to_right).start()

    def w_start(a, j):
        for k, to_right in halves(j):
            w_copy(a, k, not to_right).start()

    def sum_start(a):
        for k in (6, 7):
            @pl.loop(0, 4)
            def _(n):
                u_copy(a, k, n).start()

        o_start(a, 0)
        o_start(a, 1)
        w_start(a, 0)
        if a == 0:
            o_start(a, 2)
            w_start(a, 1)
            w_start(a, 2)

    def fold_y(a):
        for k in (6, 7):
            @pl.loop(0, 4)
            def _(n):
                u_copy(a, k, n).wait_recv()
                mine = PO.at[a, n, place(k), yh]
                mine[...] = (mine[...].astype(F32) + RV[a, k - 6, n].astype(F32)).astype(BF16)

    def combine(a, j):
        for k, to_right in halves(j):
            o_copy(a, k, to_right).wait_recv()
            mine, got = part(a, right if to_right else left, k), slot(RXO, a, k)
            mine[...] = (mine[...].astype(F32) + got[...].astype(F32)).astype(BF16)
            c_copy(a, k, to_right).start()

    def finish(a, j):
        for k, to_right in halves(j):
            w_copy(a, k, not to_right).wait_recv()
            c_copy(a, k, to_right).wait_recv()
            mine = part(a, x, k)
            mine[...] = (
                mine[...].astype(F32) + slot(RXR, a, k)[...].astype(F32) + slot(RXC, a, k)[...].astype(F32)
            ).astype(BF16)
            if k < 7:
                zz_copy(a, k).start()

    def sum_finish(a):
        for j in range(4):
            finish(a, j)

    def sum_z(a):
        for k in range(7):
            zz_copy(a, k).wait_recv()
        for s in range(2):
            total = ZR[a, 0, s].astype(F32)
            for k in range(1, 6):
                total = total + ZR[a, k, s].astype(F32)

            @pl.when(s == yh)
            def _():
                YS[a, s] = (total + ZR[a, 6, s].astype(F32) + PO[a, x, z, s].astype(F32)).astype(BF16)

            @pl.when(s != yh)
            def _():
                YS[a, s] = total.astype(BF16)

            @pl.when(jnp.logical_not(is_self(0, s)))
            def _():
                q_copy(a, s).start()

    def sum_end(a):
        for s in range(2):
            @pl.when(is_self(0, s))
            def _():
                FR[a, s] = YS[a, s]

            @pl.when(jnp.logical_not(is_self(0, s)))
            def _():
                remote(FR.at[a, s], FR.at[a, s], q_s.at[a, s], q_r.at[a, s], d_right).wait_recv()

        (bo, gi)[a][...] = (FR[a, 0].astype(F32) + FR[a, 1].astype(F32)).astype(BF16)

    def sum_drain(a):
        for k in (6, 7):
            @pl.loop(0, 4)
            def _(n):
                u_copy(a, k, n).wait_send()

        for j in range(4):
            for k, to_right in halves(j):
                o_copy(a, k, to_right).wait_send()
                w_copy(a, k, not to_right).wait_send()
                c_copy(a, k, to_right).wait_send()
                if k < 7:
                    zz_copy(a, k).wait_send()

        for s in range(2):
            @pl.when(jnp.logical_not(is_self(0, s)))
            def _():
                q_copy(a, s).wait_send()

    def columns(a, tb):
        return jnp.concatenate(
            [XT[a, xx, 2 * tb + zb, yy] for zb in range(2) for yy in range(2) for xx in range(4)], axis=0
        )

    def scatter_rows(a, tb, total):
        rounded = total.astype(BF16)
        for zb in range(2):
            for yy in range(2):
                for xx in range(4):
                    jb = zb * 8 + yy * 4 + xx
                    PO[a, xx, 2 * tb + zb, yy] = rounded[jb * FB : (jb + 1) * FB]

    def dot(a, b):
        return jnp.dot(a, b, preferred_element_type=F32)

    def weights(w):
        loads[w].wait()
        WB[w] = MW[w].astype(BF16)

        @pl.loop(0, DS // 128)
        def _(n):
            cols = pl.ds(pl.multiple_of(n * 128, 128), 128)
            WT[w, cols, :] = MW[w, :, cols].T.astype(BF16)

    def core_copy(n, src, dst):
        return remote(src, dst, d_s.at[n], d_r.at[n], d_core)

    def chip_copy(n, src, dst):
        return remote(src, dst, e_s.at[n], e_r.at[n], d_chip)

    def grad(left_op, a):
        GR[...] = jnp.zeros((HID, DS), F32)

        @pl.loop(0, 4)
        def _(tb):
            GR[...] += lax.dot_general(
                left_op[tb], columns(a, tb), (((1,), (1,)), ((), ())), preferred_element_type=F32
            )

    def adamw(w, UO, out):
        loads[3 + w].wait()
        loads[6 + w].wait()

        @pl.loop(0, FFS // 8)
        def _(n):
            rows = pl.ds(pl.multiple_of(n * 8, 8), 8)
            gradient = GR[rows, :]
            moment = beta_first * MOM[w, rows, :] + (1.0 - beta_first) * gradient
            second = beta_second * SEC[w, rows, :] + (1.0 - beta_second) * gradient * gradient
            GR[rows, :] = (moment / correct_first) / (
                jnp.sqrt(second / correct_second) + adam_epsilon
            ) + weight_decay * MW[w, rows, :]

        UO[...] = GR[0:FFS, :].astype(BF16)
        store = pltpu.make_async_copy(UO, out, lsem.at[9 + w])
        store.start()
        return store

    gather_home(0)

    for n in range(8):
        z_start(0, n)

    gather_home(1)
    gather_x(0)
    gather_step(1, 0)
    forward_far(0)
    v_start(0, far)
    gather_step(1, 1)
    forward(0, 3)
    weights(0)
    weights(1)
    gather_end(0)

    @pl.loop(0, 2)
    def _(k):
        cols = columns(0, 2 * (1 - core) + k)
        SD[k, 0] = dot(WB[0], cols)[:PAD].astype(BF16)
        SD[k, 1] = dot(WB[1], cols)[:PAD].astype(BF16)
        core_copy(8 * k, SD.at[k], RD.at[k]).start()

    @pl.loop(0, 2)
    def _(k):
        cols = columns(0, 2 * core + k)
        core_copy(8 * k, SD.at[k], RD.at[k]).wait_recv()
        gate = dot(WB[0], cols)[:PAD] + RD[k, 0].astype(F32)
        up = dot(WB[1], cols)[:PAD] + RD[k, 1].astype(F32)
        GUO[k, 0] = gate
        GUO[k, 1] = up
        SY[k, 0] = gate.astype(BF16)
        SY[k, 1] = up.astype(BF16)
        chip_copy(k, SY.at[k], RY.at[k]).start()

    gather_step(1, 2)
    weights(2)
    forward_first(1)
    gather_step(1, 3)
    forward(1, 1)

    @pl.loop(0, 2)
    def _(k):
        chip_copy(k, SY.at[k], RY.at[k]).wait_recv()
        gate_in = GUO[k, 0] + RY[k, 0].astype(F32)
        up_in = GUO[k, 1] + RY[k, 1].astype(F32)
        sig = jax.nn.sigmoid(gate_in)
        active = gate_in * sig
        ACT[k] = active
        US[k] = up_in * (sig * (1.0 + gate_in * (1.0 - sig)))
        mine = HD.at[2 * core + k]
        HD[2 * core + k, 0:PAD, :] = (active * up_in).astype(BF16)
        core_copy(1 + k, mine, mine).start()

    v_start(1, x, left, right)
    forward(1, 2)

    @pl.loop(0, 2)
    def _(k):
        theirs = HD.at[2 * (1 - core) + k]
        core_copy(1 + k, theirs, theirs).wait_recv()

    @pl.loop(0, 4)
    def _(tb):
        scatter_rows(0, tb, dot(WT[2], HD[tb]))

    forward_far(1)
    v_start(1, far)
    forward(1, 3)
    sum_start(0)
    gather_end(1)

    @pl.loop(0, 2)
    def _(k):
        SD2[k] = dot(WB[2], columns(1, 2 * (1 - core) + k))[:PAD].astype(BF16)

    core_copy(3, SD2, RD2).start()

    @pl.loop(0, 2)
    def _(k):
        DHO[k] = dot(WB[2], columns(1, 2 * core + k))[:PAD]

    core_copy(3, SD2, RD2).wait_recv()

    @pl.loop(0, 2)
    def _(k):
        DHO[k] = DHO[k] + RD2[k].astype(F32)
        SY2[k] = DHO[k].astype(BF16)
        chip_copy(2 + k, SY2.at[k], RY2.at[k]).start()

    combine(0, 0)
    combine(0, 1)
    fold_y(0)
    o_start(0, 3)
    w_start(0, 3)
    combine(0, 2)
    grad(HD, 1)
    store_down = adamw(2, UO2, ud)

    @pl.loop(0, 2)
    def _(k):
        chip_copy(2 + k, SY2.at[k], RY2.at[k]).wait_recv()
        d_hidden = DHO[k] + RY2[k].astype(F32)
        gate, up = DG.at[2 * core + k], DU.at[2 * core + k]
        DG[2 * core + k, 0:PAD, :] = (d_hidden * US[k]).astype(BF16)
        DU[2 * core + k, 0:PAD, :] = (d_hidden * ACT[k]).astype(BF16)
        core_copy(4 + k, gate, gate).start()
        core_copy(6 + k, up, up).start()

    combine(0, 3)

    @pl.loop(0, 2)
    def _(k):
        gate, up = DG.at[2 * (1 - core) + k], DU.at[2 * (1 - core) + k]
        core_copy(4 + k, gate, gate).wait_recv()
        core_copy(6 + k, up, up).wait_recv()

    @pl.loop(0, 4)
    def _(tb):
        scatter_rows(1, tb, dot(WT[0], DG[tb]) + dot(WT[1], DU[tb]))

    sum_start(1)
    sum_finish(0)
    combine(1, 0)
    o_start(1, 2)
    w_start(1, 1)
    grad(DG, 0)
    store_gate = adamw(0, UO0, ug)
    fold_y(1)
    combine(1, 1)
    o_start(1, 3)
    w_start(1, 2)
    finish(1, 0)
    sum_z(0)
    combine(1, 2)
    w_start(1, 3)
    finish(1, 1)
    grad(DU, 0)
    store_up = adamw(1, UO1, uu)
    combine(1, 3)
    finish(1, 2)
    finish(1, 3)
    sum_end(0)
    sum_z(1)
    gather_drain(0)
    gather_drain(1)
    sum_drain(0)
    for k in range(2):
        core_copy(8 * k, SD.at[k], RD.at[k]).wait_send()
    core_copy(3, SD2, RD2).wait_send()

    @pl.loop(0, 2)
    def _(k):
        hid, gate, up = HD.at[2 * core + k], DG.at[2 * core + k], DU.at[2 * core + k]
        chip_copy(k, SY.at[k], RY.at[k]).wait_send()
        chip_copy(2 + k, SY2.at[k], RY2.at[k]).wait_send()
        core_copy(1 + k, hid, hid).wait_send()
        core_copy(4 + k, gate, gate).wait_send()
        core_copy(6 + k, up, up).wait_send()

    sum_end(1)
    sum_drain(1)
    store_down.wait()
    store_gate.wait()
    store_up.wait()


def step(*inputs):
    def vmem(*shape, dtype=BF16):
        return pltpu.VMEM(shape, dtype)

    dma = pltpu.SemaphoreType.DMA
    out = jax.ShapeDtypeStruct
    shard, update = out((FB, TB), BF16), out((FFS, DS), BF16)
    in_vmem = pl.BlockSpec(memory_space=pltpu.VMEM)
    in_any = pl.BlockSpec(memory_space=pl.ANY)
    scratch = [
        vmem(2, FB, TB),
        vmem(FB, TB),
        vmem(1, ROLL, dtype=jnp.int32),
        vmem(1, ROLL, dtype=jnp.int32),
        vmem(1, TB, dtype=jnp.int32),
        vmem(2, 4, 8, 2, FB, TB),
        vmem(2, 4, 8, 2, FB, TB),
        vmem(2, 2, 4, FB, TB),
        vmem(2, 8, 2, FB, TB),
        vmem(2, 8, 2, FB, TB),
        vmem(2, 8, 2, FB, TB),
        vmem(2, 8, 2, FB, TB),
        vmem(2, 2, FB, TB),
        vmem(2, 2, FB, TB),
        vmem(3, HID, DS, dtype=F32),
        vmem(3, FFS, DS, dtype=F32),
        vmem(3, FFS, DS, dtype=F32),
        vmem(3, HID, DS),
        vmem(3, DS, HID),
        vmem(4, HID, TB),
        vmem(4, HID, TB),
        vmem(4, HID, TB),
        vmem(2, 2, PAD, TB, dtype=F32),
        vmem(2, PAD, TB, dtype=F32),
        vmem(2, PAD, TB, dtype=F32),
        vmem(2, PAD, TB, dtype=F32),
        vmem(2, 2, PAD, TB),
        vmem(2, 2, PAD, TB),
        vmem(2, 2, PAD, TB),
        vmem(2, 2, PAD, TB),
        vmem(2, PAD, TB),
        vmem(2, PAD, TB),
        vmem(2, PAD, TB),
        vmem(2, PAD, TB),
        vmem(HID, DS, dtype=F32),
        vmem(FFS, DS),
        vmem(FFS, DS),
        vmem(FFS, DS),
        dma((17,)),
        dma((2, 8, 2)), dma((2, 8, 2)),
        dma((2, 8)), dma((2, 8)),
        dma((2, 8)), dma((2, 8)),
        dma((2, 8)), dma((2, 8)),
        dma((2, 2, 4)), dma((2, 2, 4)),
        dma((2, 2, 4)), dma((2, 2, 4)),
        dma((2, 8)), dma((2, 8)),
        dma((2, 8)), dma((2, 8)),
        dma((2, 8)), dma((2, 8)),
        dma((2, 8)), dma((2, 8)),
        dma((2, 2)), dma((2, 2)),
        dma((9,)), dma((9,)),
        dma((4,)), dma((4,)),
    ]
    return pl.pallas_call(
        kernel,
        out_shape=[shard, shard, update, update, update],
        in_specs=[in_any] * 14,
        out_specs=[in_vmem] * 2 + [in_any] * 3,
        scratch_shapes=scratch,
        compiler_params=pltpu.CompilerParams(
            collective_id=0, has_side_effects=True, vmem_limit_bytes=58 * 1024 * 1024
        ),
        cost_estimate=pl.CostEstimate(flops=5_100_000_000, bytes_accessed=12_000_000, transcendentals=1_000_000),
        name="fused_step",
    )(*inputs)


def handing_on(*refs):
    arrays, results, held, sems = refs[:5], refs[5:10], refs[10:15], refs[15]
    fetches = [pltpu.make_async_copy(a, h, sems.at[0, n]) for n, (a, h) in enumerate(zip(arrays, held))]
    stores = [pltpu.make_async_copy(h, r, sems.at[1, n]) for n, (h, r) in enumerate(zip(held, results))]
    for fetch in fetches:
        fetch.start()
    for fetch, store in zip(fetches, stores):
        fetch.wait()
        store.start()
    for store in stores:
        store.wait()


def hand_on(*results):
    in_any = pl.BlockSpec(memory_space=pl.ANY)
    return pl.pallas_call(
        handing_on,
        out_shape=[jax.ShapeDtypeStruct(r.shape, r.dtype) for r in results],
        in_specs=[in_any] * 5,
        out_specs=[in_any] * 5,
        scratch_shapes=[pltpu.VMEM(r.shape, r.dtype) for r in results] + [pltpu.SemaphoreType.DMA((2, 5))],
        compiler_params=pltpu.CompilerParams(vmem_limit_bytes=58 * 1024 * 1024),
        name="hand_on",
    )(*results)


def body(tokens, cotangent, pass_counts, group_ids, token_rollout, *states):
    results = step(
        tokens.T,
        cotangent.T,
        pass_counts.reshape(1, ROLL),
        group_ids.reshape(1, ROLL),
        token_rollout.reshape(1, TB),
        *states,
    )
    block_out, grad_input, update_gate, update_up, update_down = hand_on(*results)
    return block_out.T, grad_input.T, update_gate, update_up, update_down


def solution(mesh):
    act, rep, weight = P("dp", "fsdp"), P(), P("fsdp", "dp")
    return jax.shard_map(
        body,
        mesh=mesh,
        in_specs=(act, act, rep, rep, P("dp")) + (weight,) * 9,
        out_specs=(act, act, weight, weight, weight),
        check_vma=False,
    )
```
